128 devices in a mesh: row: 16 (over z, y_hi, core), col: 8 (over x, y_lo).
Axes of the slice: x: 4, y: 4 (y_hi: 2, y_lo: 2; y = y_hi * 2 + y_lo), z: 4, core: 2. Of those that a mesh axis runs over, the one named last changes fastest.
Arguments:
- source_embed: bfloat16 [40, 24576], P(None, ('row', 'col')), may hold values from -4 to 4
- target_embed: bfloat16 [40, 24576], P(None, ('row', 'col')), may hold values from -4 to 4
- features: bfloat16 [24576, 128], P(('row', 'col')), may hold values from -6 to 6
- cotangent: bfloat16 [24576, 128], P(('row', 'col')), may hold values from -6 to 6
Outputs:
- hop_output: bfloat16 [24576, 128], P(('row', 'col'))
- grad_features: bfloat16 [24576, 128], P(('row', 'col'))
- grad_source: float32 [40, 24576], P(None, ('row', 'col'))
- grad_target: float32 [40, 24576], P(None, ('row', 'col'))
The draws below stay inside these ranges and needn't reach their ends.
All inputs are finite; a program needn't handle non-finite values.
Results may differ from the reference program's by a relative error of at most 0.015.
Values may be sent and summed in bfloat16 or wider, within the bound.
No kernel may reach another device: no remote copies, remote signals or barrier semaphores. Data moves between devices by JAX's collectives and lax.ppermute only.
A program may use at most 64 MiB of HBM per device.

```python
import math
import jax
import jax.numpy as jnp
from jax import lax

EMB = 40
FEAT = 128
NODES = 24576


def draw_source_embed(key, part):
    key = jax.random.fold_in(key, 11)
    values = jnp.clip(jax.random.normal(key, (EMB, NODES), jnp.float32) * 0.75, -4.0, 4.0)
    return values.astype(jnp.bfloat16)


def draw_target_embed(key, part):
    key = jax.random.fold_in(key, 13)
    values = jnp.clip(jax.random.normal(key, (EMB, NODES), jnp.float32) * 0.75, -4.0, 4.0)
    return values.astype(jnp.bfloat16)


def block_scale(own_key, dims, pieces, smallest, largest):
    def one(position, blocks):
        draws = jax.random.uniform(jax.random.fold_in(jax.random.fold_in(own_key, 6), position), (blocks,), jnp.float32, smallest / len(pieces), largest / len(pieces))
        return jnp.repeat(jnp.exp(draws), dims[position] // blocks).reshape((-1,) + (1,) * (len(dims) - position - 1))

    factor_of = one(*pieces[0])
    for cut in pieces[1:]:
        factor_of = factor_of * one(*cut)
    return factor_of


def bell_draw(own_key, shape, spread, most, cuts=(), kind=jnp.bfloat16):
    values = spread * jax.random.normal(own_key, shape, jnp.float32)
    if cuts:
        values = values * block_scale(own_key, shape, cuts, -0.22, 0.18)
    return jnp.clip(values, -most, most).astype(kind)


def setup_inputs(seed: int = 0) -> dict:
    key_list = jax.random.split(jax.random.key(seed), 5)
    source_embed = draw_source_embed(jax.random.fold_in(key_list[4], 71), 0)
    target_embed = draw_target_embed(jax.random.fold_in(key_list[4], 71), 0)
    features = bell_draw(key_list[2], (NODES, FEAT), 1.0, 6.0, ((0, 128),))
    cotangent = bell_draw(key_list[3], (NODES, FEAT), 1.0, 6.0, ((0, 128),))
    return {"source_embed": source_embed, "target_embed": target_embed, "features": features, "cotangent": cotangent}


def reference(source_embed, target_embed, features, cotangent):
    node_count = features.shape[0]
    feat_count = features.shape[1]
    emb_count = source_embed.shape[0]
    block_rows = math.gcd(node_count, 1024)
    block_count = node_count // block_rows

    def block_step(carry, block_index):
        reverse_hop, reverse_grad, target_grad = carry
        first_row = block_index * block_rows
        source_block = lax.dynamic_slice_in_dim(source_embed, first_row, block_rows, 1)
        feat_block = lax.dynamic_slice_in_dim(features, first_row, block_rows, 0)
        cot_block = lax.dynamic_slice_in_dim(cotangent, first_row, block_rows, 0)
        scores = lax.dot_general(source_block, target_embed, (((0,), (0,)), ((), ())), preferred_element_type=jnp.float32)
        positive = jnp.maximum(scores, 0.0)
        row_peak = jnp.max(positive, axis=1, keepdims=True)
        lifted = jnp.exp(positive - row_peak)
        row_total = jnp.sum(lifted, axis=1, keepdims=True)
        soft = lifted / row_total
        soft_half = soft.astype(jnp.bfloat16)
        forward_hop = jnp.dot(soft_half, features, preferred_element_type=jnp.float32)
        reverse_hop = reverse_hop + lax.dot_general(soft_half, feat_block, (((0,), (0,)), ((), ())), preferred_element_type=jnp.float32)
        outer_grad = lax.dot_general(cot_block, features, (((1,), (1,)), ((), ())), preferred_element_type=jnp.float32)
        outer_grad = outer_grad + lax.dot_general(feat_block, cotangent, (((1,), (1,)), ((), ())), preferred_element_type=jnp.float32)
        row_delta = jnp.sum(soft * outer_grad, axis=1, keepdims=True)
        score_grad = jnp.where(scores > 0.0, soft * (outer_grad - row_delta), 0.0)
        score_half = score_grad.astype(jnp.bfloat16)
        forward_grad = jnp.dot(soft_half, cotangent, preferred_element_type=jnp.float32)
        reverse_grad = reverse_grad + lax.dot_general(soft_half, cot_block, (((0,), (0,)), ((), ())), preferred_element_type=jnp.float32)
        source_grad = lax.dot_general(target_embed, score_half, (((1,), (1,)), ((), ())), preferred_element_type=jnp.float32)
        target_grad = target_grad + jnp.dot(source_block, score_half, preferred_element_type=jnp.float32)
        return (reverse_hop, reverse_grad, target_grad), (forward_hop, forward_grad, source_grad)

    start_carry = (jnp.zeros((node_count, feat_count), jnp.float32),
                   jnp.zeros((node_count, feat_count), jnp.float32),
                   jnp.zeros((emb_count, node_count), jnp.float32))
    carry, stacked = lax.scan(block_step, start_carry, jnp.arange(block_count, dtype=jnp.int32))
    reverse_hop, reverse_grad, target_grad = carry
    forward_hop = stacked[0].reshape(node_count, feat_count)
    forward_grad = stacked[1].reshape(node_count, feat_count)
    source_grad = jnp.transpose(stacked[2], (1, 0, 2)).reshape(emb_count, node_count)
    hop_output = (forward_hop + reverse_hop).astype(jnp.bfloat16)
    grad_features = (forward_grad + reverse_grad).astype(jnp.bfloat16)
    return hop_output, grad_features, source_grad, target_grad
```

```python
import functools

import jax
import jax.numpy as jnp
import numpy as np
from jax import lax
from jax.experimental import pallas as pl
from jax.experimental.pallas import tpu as pltpu
from jax.sharding import PartitionSpec as P

F32 = jnp.float32
BF16 = jnp.bfloat16
LANES = 128
VMEM_MIB = 24
SMEM = pl.BlockSpec(memory_space=pltpu.SMEM)
MOVES = (0, 1, 2, -1)


def pick(total, unit, most):
    size = total
    while size > most or total % size or size % unit:
        size -= unit
    return size


def whole(shape):
    return pl.BlockSpec(shape, lambda *i: (0,) * len(shape))


def shapes(*pairs):
    return [jax.ShapeDtypeStruct(shape, kind) for shape, kind in pairs]


def params(mib=VMEM_MIB):
    return pltpu.CompilerParams(vmem_limit_bytes=mib * 1024 * 1024)


def places(row_size, col_size):
    depth, width = row_size // 4, col_size // 2
    table = np.zeros((row_size * col_size, 16), np.int32)
    for index in range(row_size * col_size):
        row, col = divmod(index, col_size)
        slots = [(col // 2 + move) % width for move in MOVES] + [(row // 4 + move) % depth for move in MOVES]
        table[index, :12] = slots + [col % 2, row // 2 % 2, col, col // 2]
    return table


def assemble(own, chunk_refs, place_ref, base, parity, pair_ref, turned_ref, nodes_ref):
    extra = chunk_refs[0].shape[1] - own
    even = parity == 0
    blank = jnp.zeros((extra, 2 * own - chunk_refs[0].shape[2]), F32)
    for slot, chunk_ref in enumerate(chunk_refs):
        start = place_ref[base + slot] * 2 * own
        for flip in range(2):
            rows = pl.ds(pl.multiple_of(start + (parity ^ flip) * own, 64), own)
            pair_ref[rows, :] = chunk_ref[flip, :own, :]
        first = chunk_ref[0, own:, :].astype(F32)
        second = chunk_ref[1, own:, :].astype(F32)
        left = jnp.concatenate([jnp.where(even, first, second), blank], axis=1)
        right = jnp.concatenate([blank, jnp.where(even, second, first)], axis=1)
        both = left + pltpu.roll(right, own - blank.shape[1], 1)
        turned_ref[:extra, pl.ds(pl.multiple_of(start, LANES), 2 * own)] = both.astype(BF16)
    turned_ref[extra:, :] = jnp.zeros((LANES - extra, turned_ref.shape[1]), BF16)
    nodes_ref[...] = jnp.transpose(turned_ref[...])


def stats_kernel(own, feat, place_ref, *rest):
    parts = len(MOVES)
    a_refs, b0_refs, b1_refs = rest[0 : 2 * parts : 2], rest[1 : 2 * parts : 2], rest[2 * parts : 3 * parts]
    scaled_ref, stats_ref, a_pair, a_pair_t, a_src, a_src_t, b_pair, b_dst, b_dst_t, scores, peaks = rest[3 * parts :]
    step = pl.program_id(0)
    last = pl.num_programs(0) - 1
    count, cols = scores.shape
    span = pick(cols, LANES, 1024)
    repeat = span // LANES

    def tiles(array):
        return [array[:, lane : lane + LANES] for lane in range(0, span, LANES)]

    def work(ahead, behind):
        block = step - 1 if behind else step
        here = pl.ds(pl.multiple_of(block * count, count), count)
        there = pl.ds(pl.multiple_of(step * count, count), count)
        total = jnp.zeros((count, LANES), F32)
        peak = jnp.zeros((count, LANES), F32)
        sums = jnp.zeros((count, 2 * feat), F32)
        for start in range(0, cols, span):
            part = slice(start, start + span)
            if behind:
                before = peaks[...]
                half = jnp.exp(scores[:, part] - jnp.concatenate([before] * repeat, axis=1)).astype(BF16)
                total = total + sum(tiles(half.astype(F32)))
                sums = sums + jnp.dot(half, b_pair[part, :], preferred_element_type=F32)
            if ahead:
                fresh = jnp.maximum(jnp.dot(a_src[there, :], b_dst_t[:, part], preferred_element_type=F32), 0.0)
                scores[:, part] = fresh
                peak = functools.reduce(jnp.maximum, tiles(fresh), peak)
        if behind:
            total = jnp.sum(total, axis=1, keepdims=True)
            sums = sums / total
            scaled_ref[...] = sums.astype(BF16)
            mates = a_pair[here, :].astype(F32)
            inner = jnp.sum(sums[:, :feat] * mates[:, feat:] + sums[:, feat:] * mates[:, :feat], axis=1, keepdims=True)
            lane = lax.broadcasted_iota(jnp.int32, (count, LANES), 1)
            table = jnp.where(lane == 0, peaks[...], jnp.where(lane == 1, total, inner))
            stats_ref[...] = jnp.broadcast_to(jnp.transpose(table)[:4][None], stats_ref.shape)
        if ahead:
            peaks[...] = jnp.broadcast_to(jnp.max(peak, axis=1, keepdims=True), peaks.shape)

    @pl.when(step == 0)
    def _():
        assemble(own, a_refs, place_ref, 0, place_ref[8], a_pair, a_src_t, a_src)
        half = b_pair.shape[0] // 2
        for index, b_refs in enumerate((b0_refs, b1_refs)):
            part = pl.ds(index * half, half)
            outs = (b_pair.at[part, :], b_dst_t.at[:, part], b_dst.at[part, :])
            assemble(own, b_refs, place_ref, 4, place_ref[9], *outs)
        a_pair_t[:feat] = jnp.transpose(a_pair[:, feat:])
        a_pair_t[feat:] = jnp.transpose(a_pair[:, :feat])
        work(True, False)

    @pl.when((step > 0) & (step < last))
    def _():
        work(True, True)

    @pl.when(step == last)
    def _():
        work(False, True)


def row_stats(place, a_parts, b0_parts, b1_parts, own, feat):
    mates = sum(part.shape[0] for part in a_parts)
    rows = mates * own
    cols = 2 * own * sum(part.shape[0] for part in b0_parts)
    pair = 2 * feat
    step = pick(rows, LANES, 256)
    kept = [((rows, pair), BF16), ((pair, rows), BF16), ((rows, LANES), BF16), ((LANES, rows), BF16)]
    kept += [((cols, pair), BF16), ((cols, LANES), BF16), ((LANES, cols), BF16)]
    parts = [part for both in zip(a_parts, b0_parts) for part in both] + b1_parts
    scaled, stats, *kept = pl.pallas_call(
        functools.partial(stats_kernel, own, feat),
        grid=(rows // step + 1,),
        in_specs=[SMEM] + [whole(x.shape) for x in parts],
        out_specs=[
            pl.BlockSpec((step, pair), lambda i: (jnp.maximum(i - 1, 0), 0)),
            pl.BlockSpec((mates, 4, step), lambda i: (0, 0, jnp.maximum(i - 1, 0))),
        ]
        + [whole(shape) for shape, kind in kept],
        out_shape=shapes(((rows, pair), BF16), ((mates, 4, rows), F32), *kept),
        scratch_shapes=[pltpu.VMEM((step, cols), F32), pltpu.VMEM((step, LANES), F32)],
        compiler_params=params(),
        cost_estimate=pl.CostEstimate(flops=2 * rows * cols * 512, bytes_accessed=8 << 20, transcendentals=rows * cols),
        name="row_stats",
    )(place, *parts)
    return scaled, stats, kept


def tile_kernel(
    own, feat, last, place_ref, a_pair, a_pair_t, a_src, a_src_t, b_pair, b_dst, b_dst_t, stats_ref, *rest
):
    pair = 2 * feat
    step = pl.program_id(0)
    if last:
        start_ref, mine_ref, cols_ref, source_ref, *piece_refs, twin_ref, table, slots = rest
    else:
        scaled_ref, cols_ref, source_ref, mine_ref, given_ref, table, weights_ref = rest
    extra = cols_ref.shape[1] - own

    @pl.when(step == 0)
    def _():
        source_ref[...] = start_ref[...] if last else jnp.zeros_like(source_ref)
        stats = stats_ref[...]
        peaks = stats[:, 0:1]
        peak = jnp.max(peaks, axis=0)
        weights = jnp.exp(peaks - peak[None]) * stats[:, 1:2]
        total = jnp.sum(weights, axis=0)
        table[0:1, :] = peak + jnp.log(total)
        table[1:2, :] = jnp.sum(weights * stats[:, 2:3], axis=0) / total
        if not last:
            at = place_ref[10]
            weight = jnp.exp(stats_ref[at, 0:1] - peak) * stats_ref[at, 1:2] / total
            weights_ref[...] = jnp.transpose(jnp.broadcast_to(weight, (LANES, weight.shape[1])))
            for slot in range(mine_ref.shape[0]):
                for flip, out_ref in enumerate((mine_ref, given_ref)):
                    chunk = 2 * (place_ref[11] ^ slot) + (place_ref[8] ^ flip)
                    rows = pl.ds(pl.multiple_of(chunk * own, 64), own)
                    out_ref[slot] = (weights_ref[rows, 0:1] * scaled_ref[rows, :].astype(F32)).astype(BF16)

    scores = jnp.dot(b_dst[...], a_src_t[...], preferred_element_type=F32)
    outer = jnp.dot(b_pair[...], a_pair_t[...], preferred_element_type=F32)
    soft = jnp.exp(jnp.maximum(scores, 0.0) - table[0:1, :])
    grad = jnp.where(scores > 0.0, soft * (outer - table[1:2, :]), 0.0)
    soft_half = soft.astype(BF16)
    grad_half = grad.astype(BF16)
    col_sums = jnp.dot(soft_half, a_pair[...], preferred_element_type=F32).astype(BF16)
    target_sums = jnp.dot(grad_half, a_src[...], preferred_element_type=F32)
    for slot in range(cols_ref.shape[0]):
        rows = slice(slot * own, (slot + 1) * own)
        cols_ref[slot, :own, :] = col_sums[rows]
        wide = jnp.concatenate([target_sums[rows], jnp.zeros((pair - own, LANES), F32)], axis=0)
        cols_ref[slot, own:, :] = jnp.transpose(wide)[:extra].astype(BF16)
    source_ref[...] += jnp.dot(b_dst_t[:extra], grad_half, preferred_element_type=F32)

    if last:

        @pl.when(step == pl.num_programs(0) - 1)
        def _():
            fill = jnp.zeros((extra, pair - own), F32)
            for chunk in range(slots.shape[0]):
                part = source_ref[:, chunk * own : (chunk + 1) * own]
                slots[place_ref[10] ^ chunk] = jnp.concatenate([part, fill], axis=1)
            for slot, piece_ref in enumerate(piece_refs):
                piece_ref[:own, :] = mine_ref[slot]
                piece_ref[own:, :] = slots[2 * slot].astype(BF16)
                twin_ref[slot] = slots[2 * slot + 1].astype(BF16)


def tile_sums(place, kept, half, stats, late, own, feat, extra, last, name):
    rows, pair = kept[0].shape
    cols = kept[4].shape[0] // 2
    mates = stats.shape[0]
    step = pick(cols, 2 * own, 2 * own)
    base = half * (cols // step)
    scratch = [pltpu.VMEM((8, rows), F32)]
    if last:
        kinds = [((own + extra, pair), BF16)] * (mates // 2) + [((mates // 2, extra, pair), BF16)]
        scratch += [pltpu.VMEM((mates, extra, pair), F32)]
    else:
        kinds = [((mates // 2, own, pair), BF16)] * 2
        scratch += [pltpu.VMEM((rows, LANES), F32)]
    return pl.pallas_call(
        functools.partial(tile_kernel, own, feat, last),
        grid=(cols // step,),
        in_specs=[
            SMEM,
            *[whole(x.shape) for x in kept[:4]],
            pl.BlockSpec((step, pair), lambda i: (i + base, 0)),
            pl.BlockSpec((step, LANES), lambda i: (i + base, 0)),
            pl.BlockSpec((LANES, step), lambda i: (0, i + base)),
            *[whole(x.shape) for x in (stats, *late)],
        ],
        out_specs=[pl.BlockSpec((step // own, own + extra, pair), lambda i: (i, 0, 0)), whole((extra, rows))]
        + [whole(shape) for shape, kind in kinds],
        out_shape=shapes(((cols // own, own + extra, pair), BF16), ((extra, rows), F32), *kinds),
        scratch_shapes=scratch,
        compiler_params=params(),
        cost_estimate=pl.CostEstimate(flops=2 * rows * cols * 1280, bytes_accessed=8 << 20, transcendentals=rows * cols),
        name=name,
    )(place, *kept, stats, *late)


def join_cols_kernel(own_ref, other_ref, out_ref):
    out_ref[...] = (own_ref[...].astype(F32) + other_ref[...].astype(F32)).astype(BF16)


def join_rows_kernel(given_ref, twin_ref, *rest):
    count, own = given_ref.shape[:2]
    for slot, (piece_ref, out_ref) in enumerate(zip(rest[:count], rest[count:])):
        out_ref[:own, :] = (piece_ref[:own, :].astype(F32) + given_ref[slot].astype(F32)).astype(BF16)
        out_ref[own:, :] = (piece_ref[own:, :].astype(F32) + twin_ref[slot].astype(F32)).astype(BF16)


def join(kernel, name, outs, *arrays):
    return pl.pallas_call(
        kernel,
        out_shape=[jax.ShapeDtypeStruct(out.shape, out.dtype) for out in outs],
        compiler_params=params(8),
        name=name,
    )(*arrays)


def finish_kernel(own, feat, emb_count, cols_ref, *rest):
    piece_refs, (hop_ref, grad_ref, source_ref, target_ref) = rest[:-4], rest[-4:]
    total = jnp.zeros((own, 2 * feat), F32)
    extra = jnp.zeros((cols_ref.shape[1] - own, 2 * feat), F32)
    source = extra
    for piece_ref in piece_refs:
        total = total + piece_ref[:own, :].astype(F32)
        source = source + piece_ref[own:, :].astype(F32)
    for slot in range(cols_ref.shape[0]):
        total = total + cols_ref[slot, :own, :].astype(F32)
        extra = extra + cols_ref[slot, own:, :].astype(F32)
    hop_ref[...] = total[:, :feat].astype(BF16)
    grad_ref[...] = total[:, feat:].astype(BF16)
    source_ref[...] = source[:emb_count, :own]
    target_ref[...] = extra[:emb_count, :own]


def finish(cols, pieces, own, feat, emb_count):
    return pl.pallas_call(
        functools.partial(finish_kernel, own, feat, emb_count),
        out_shape=shapes(
            ((own, feat), BF16), ((own, feat), BF16), ((emb_count, own), F32), ((emb_count, own), F32)
        ),
        compiler_params=params(8),
        name="finish",
    )(cols, *pieces)


def local(sizes, source_embed, target_embed, features, cotangent):
    row_size, col_size = sizes
    emb_count, own = source_embed.shape
    feat = features.shape[1]
    pair = 2 * feat
    extra = -(-emb_count // 16) * 16
    depth, width = row_size // 4, col_size // 2
    both = ("row", "col")

    def device(z, y, core, x, skew):
        return (((z % depth) * 2 + y) * 2 + core) * col_size + (x % width) * 2 + (skew ^ y)

    groups = [
        [device(z, y, core, x, skew) for z in range(depth) for y in range(2)]
        for core in range(2) for x in range(width) for skew in range(2)
    ]

    def mate(array, bits):
        return lax.ppermute(array, "col", [(c, c ^ bits) for c in range(col_size)])

    def swap(array):
        return lax.ppermute(array, "row", [(r, r ^ 1) for r in range(row_size)])

    def along_x(array, move, flip):
        pairs = [(x * 2 + y, ((x + move) % width) * 2 + (y ^ flip)) for x in range(width) for y in range(2)]
        return lax.ppermute(array, "col", pairs)

    def along_z(array, move, flip):
        pairs = [
            (device(z, y, core, x, skew), device(z + move, y ^ flip, core, x, skew))
            for z in range(depth) for y in range(2) for core in range(2) for x in range(width) for skew in range(2)
        ]
        return lax.ppermute(array, both, pairs)

    def pack(embed):
        left = jnp.pad(features, ((0, extra), (0, feat)))
        right = jnp.pad(cotangent, ((0, extra), (feat, 0)))
        return left + right + jnp.pad(embed, ((own, extra - emb_count), (0, pair - own)))

    index = lax.axis_index(both)
    place = lax.dynamic_index_in_dim(jnp.asarray(places(row_size, col_size)), index, 0, keepdims=False)
    chunks, alongs = (pack(target_embed), pack(source_embed)), (along_z, along_x)
    near = [jnp.stack([chunk, along(chunk, 0, 1)]) for chunk, along in zip(chunks, alongs)]
    near, place = lax.optimization_barrier((near, place))
    moved = [[along(array, -move, 0) for array, along in zip(near, alongs)] for move in MOVES[1:]]
    b_parts, a_parts = [[array, *[pair[index] for pair in moved]] for index, array in enumerate(near)]
    others = [swap(part) for part in b_parts]
    scaled, stats, kept = row_stats(place, a_parts, b_parts, others, own, feat)
    stats = lax.all_to_all(stats, "col", 0, 0)

    sizes = (own, feat, extra)
    other_cols, start, mine, given = tile_sums(place, kept, 1, stats, (scaled,), *sizes, False, "other_tile")
    other_cols = swap(other_cols)
    given = mate(given, 1)
    own_cols, unused, *pieces, twin = tile_sums(place, kept, 0, stats, (start, mine), *sizes, True, "own_tile")
    twin = mate(twin, 1)
    (cols,) = join(join_cols_kernel, "join_cols", [own_cols], own_cols, other_cols)
    cols = lax.all_to_all(cols, both, 0, 0, axis_index_groups=groups)
    pieces = join(join_rows_kernel, "join_rows", pieces, given, twin, *pieces)
    pieces = [mate(piece, 2 * slot) if slot else piece for slot, piece in enumerate(pieces)]
    return tuple(finish(cols, pieces, own, feat, emb_count))


def solution(mesh):
    nodes = P(("row", "col"), None)
    embeds = P(None, ("row", "col"))
    sizes = (mesh.shape["row"], mesh.shape["col"])
    return jax.shard_map(
        functools.partial(local, sizes),
        mesh=mesh,
        in_specs=(embeds, embeds, nodes, nodes),
        out_specs=(nodes, nodes, embeds, embeds),
        check_vma=False,
    )
```

```python
import functools

import jax
import jax.numpy as jnp
import numpy as np
from jax import lax
from jax.experimental import pallas as pl
from jax.experimental.pallas import tpu as pltpu
from jax.sharding import PartitionSpec as P

F32 = jnp.float32
BF16 = jnp.bfloat16
LANES = 128
VMEM_MIB = 24
SMEM = pl.BlockSpec(memory_space=pltpu.SMEM)
MOVES = (0, 1, 2, -1)


def pick(total, unit, most):
    size = total
    while size > most or total % size or size % unit:
        size -= unit
    return size


def whole(shape):
    return pl.BlockSpec(shape, lambda *i: (0,) * len(shape))


def shapes(*pairs):
    return [jax.ShapeDtypeStruct(shape, kind) for shape, kind in pairs]


def params(mib=VMEM_MIB):
    return pltpu.CompilerParams(vmem_limit_bytes=mib * 1024 * 1024)


def places(row_size, col_size):
    depth, width = row_size // 4, col_size // 2
    table = np.zeros((row_size * col_size, 16), np.int32)
    for index in range(row_size * col_size):
        row, col = divmod(index, col_size)
        slots = [(col // 2 + move) % width for move in MOVES] + [(row // 4 + move) % depth for move in MOVES]
        table[index, :12] = slots + [col % 2, row // 2 % 2, col, col // 2]
    return table


def assemble(own, chunk_refs, place_ref, base, parity, pair_ref, turned_ref, nodes_ref):
    extra = chunk_refs[0].shape[1] - own
    even = parity == 0
    blank = jnp.zeros((extra, 2 * own - chunk_refs[0].shape[2]), F32)
    for slot, chunk_ref in enumerate(chunk_refs):
        start = place_ref[base + slot] * 2 * own
        for flip in range(2):
            rows = pl.ds(pl.multiple_of(start + (parity ^ flip) * own, 64), own)
            pair_ref[rows, :] = chunk_ref[flip, :own, :]
        first = chunk_ref[0, own:, :].astype(F32)
        second = chunk_ref[1, own:, :].astype(F32)
        left = jnp.concatenate([jnp.where(even, first, second), blank], axis=1)
        right = jnp.concatenate([blank, jnp.where(even, second, first)], axis=1)
        both = left + pltpu.roll(right, own - blank.shape[1], 1)
        turned_ref[:extra, pl.ds(pl.multiple_of(start, LANES), 2 * own)] = both.astype(BF16)
    turned_ref[extra:, :] = jnp.zeros((LANES - extra, turned_ref.shape[1]), BF16)
    nodes_ref[...] = jnp.transpose(turned_ref[...])


def stats_kernel(own, feat, place_ref, *rest):
    parts = len(MOVES)
    a_refs, b0_refs, b1_refs = rest[0 : 2 * parts : 2], rest[1 : 2 * parts : 2], rest[2 * parts : 3 * parts]
    scaled_ref, stats_ref, a_pair, a_pair_t, a_src, a_src_t, b_pair, b_dst, b_dst_t, scores, peaks = rest[3 * parts :]
    step = pl.program_id(0)
    last = pl.num_programs(0) - 1
    count, cols = scores.shape
    span = pick(cols, LANES, 512)
    repeat = span // LANES

    def tiles(array):
        return [array[:, lane : lane + LANES] for lane in range(0, span, LANES)]

    def work(ahead, behind):
        block = step - 1 if behind else step
        here = pl.ds(pl.multiple_of(block * count, count), count)
        there = pl.ds(pl.multiple_of(step * count, count), count)
        total = jnp.zeros((count, LANES), F32)
        peak = jnp.zeros((count, LANES), F32)
        sums = jnp.zeros((count, 2 * feat), F32)
        for start in range(0, cols, span):
            part = slice(start, start + span)
            if behind:
                before = peaks[...]
                half = jnp.exp(scores[:, part] - jnp.concatenate([before] * repeat, axis=1)).astype(BF16)
                total = total + sum(tiles(half.astype(F32)))
                sums = sums + jnp.dot(half, b_pair[part, :], preferred_element_type=F32)
            if ahead:
                fresh = jnp.maximum(jnp.dot(a_src[there, :], b_dst_t[:, part], preferred_element_type=F32), 0.0)
                scores[:, part] = fresh
                peak = functools.reduce(jnp.maximum, tiles(fresh), peak)
        if behind:
            total = jnp.sum(total, axis=1, keepdims=True)
            sums = sums / total
            scaled_ref[...] = sums.astype(BF16)
            mates = a_pair[here, :].astype(F32)
            inner = jnp.sum(sums[:, :feat] * mates[:, feat:] + sums[:, feat:] * mates[:, :feat], axis=1, keepdims=True)
            lane = lax.broadcasted_iota(jnp.int32, (count, LANES), 1)
            table = jnp.where(lane == 0, peaks[...], jnp.where(lane == 1, total, inner))
            stats_ref[...] = jnp.broadcast_to(jnp.transpose(table)[:4][None], stats_ref.shape)
        if ahead:
            peaks[...] = jnp.broadcast_to(jnp.max(peak, axis=1, keepdims=True), peaks.shape)

    @pl.when(step == 0)
    def _():
        assemble(own, a_refs, place_ref, 0, place_ref[8], a_pair, a_src_t, a_src)
        half = b_pair.shape[0] // 2
        for index, b_refs in enumerate((b0_refs, b1_refs)):
            part = pl.ds(index * half, half)
            outs = (b_pair.at[part, :], b_dst_t.at[:, part], b_dst.at[part, :])
            assemble(own, b_refs, place_ref, 4, place_ref[9], *outs)
        a_pair_t[:feat] = jnp.transpose(a_pair[:, feat:])
        a_pair_t[feat:] = jnp.transpose(a_pair[:, :feat])
        work(True, False)

    @pl.when((step > 0) & (step < last))
    def _():
        work(True, True)

    @pl.when(step == last)
    def _():
        work(False, True)


def row_stats(place, a_parts, b0_parts, b1_parts, own, feat):
    mates = sum(part.shape[0] for part in a_parts)
    rows = mates * own
    cols = 2 * own * sum(part.shape[0] for part in b0_parts)
    pair = 2 * feat
    step = pick(rows, LANES, 512)
    kept = [((rows, pair), BF16), ((pair, rows), BF16), ((rows, LANES), BF16), ((LANES, rows), BF16)]
    kept += [((cols, pair), BF16), ((cols, LANES), BF16), ((LANES, cols), BF16)]
    parts = [part for both in zip(a_parts, b0_parts) for part in both] + b1_parts
    scaled, stats, *kept = pl.pallas_call(
        functools.partial(stats_kernel, own, feat),
        grid=(rows // step + 1,),
        in_specs=[SMEM] + [whole(x.shape) for x in parts],
        out_specs=[
            pl.BlockSpec((step, pair), lambda i: (jnp.maximum(i - 1, 0), 0)),
            pl.BlockSpec((mates, 4, step), lambda i: (0, 0, jnp.maximum(i - 1, 0))),
        ]
        + [whole(shape) for shape, kind in kept],
        out_shape=shapes(((rows, pair), BF16), ((mates, 4, rows), F32), *kept),
        scratch_shapes=[pltpu.VMEM((step, cols), F32), pltpu.VMEM((step, LANES), F32)],
        compiler_params=params(),
        cost_estimate=pl.CostEstimate(flops=2 * rows * cols * 512, bytes_accessed=8 << 20, transcendentals=rows * cols),
        name="row_stats",
    )(place, *parts)
    return scaled, stats, kept


def weigh_kernel(own, place_ref, stats_ref, scaled_ref, table_ref, mine_ref, given_ref, weights_ref):
    stats = stats_ref[...]
    peaks = stats[:, 0:1]
    peak = jnp.max(peaks, axis=0)
    weights = jnp.exp(peaks - peak[None]) * stats[:, 1:2]
    total = jnp.sum(weights, axis=0)
    table_ref[0:1, :] = peak + jnp.log(total)
    table_ref[1:2, :] = jnp.sum(weights * stats[:, 2:3], axis=0) / total
    table_ref[2:, :] = jnp.zeros((table_ref.shape[0] - 2, table_ref.shape[1]), F32)
    at = place_ref[10]
    weight = jnp.exp(stats_ref[at, 0:1] - peak) * stats_ref[at, 1:2] / total
    weights_ref[...] = jnp.transpose(jnp.broadcast_to(weight, (LANES, weight.shape[1])))
    for slot in range(mine_ref.shape[0]):
        for flip, out_ref in enumerate((mine_ref, given_ref)):
            chunk = 2 * (place_ref[11] ^ slot) + (place_ref[8] ^ flip)
            rows = pl.ds(pl.multiple_of(chunk * own, 64), own)
            out_ref[slot] = (weights_ref[rows, 0:1] * scaled_ref[rows, :].astype(F32)).astype(BF16)


def weigh(place, stats, scaled, own):
    rows, pair = scaled.shape
    part = ((stats.shape[0] // 2, own, pair), BF16)
    return pl.pallas_call(
        functools.partial(weigh_kernel, own),
        in_specs=[SMEM] + [pl.BlockSpec(memory_space=pltpu.VMEM)] * 2,
        out_shape=shapes(((8, rows), F32), part, part),
        scratch_shapes=[pltpu.VMEM((rows, LANES), F32)],
        compiler_params=params(8),
        name="weigh",
    )(place, stats, scaled)


def tile_kernel(
    own, feat, last, place_ref, a_pair, a_pair_t, a_src, a_src_t, b_pair, b_dst, b_dst_t, table, *rest
):
    pair = 2 * feat
    step = pl.program_id(0)
    end = pl.num_programs(0) - 1
    if last:
        start_ref, mine_ref, cols_ref, source_ref, *piece_refs, twin_ref, scores, outer, slots = rest
    else:
        cols_ref, source_ref, scores, outer = rest
    extra = cols_ref.shape[1] - own
    count, rows = scores.shape
    span = pick(rows, LANES, 256)

    def work(ahead, behind):
        col_sums = jnp.zeros((count, pair), F32)
        target_sums = jnp.zeros((count, LANES), F32)
        for start in range(0, rows, span):
            part = slice(start, start + span)
            if behind:
                score = scores[:, part]
                soft = jnp.exp(jnp.maximum(score, 0.0) - table[0:1, part])
                grad = jnp.where(score > 0.0, soft * (outer[:, part] - table[1:2, part]), 0.0)
                soft_half = soft.astype(BF16)
                grad_half = grad.astype(BF16)
                col_sums = col_sums + jnp.dot(soft_half, a_pair[part, :], preferred_element_type=F32)
                target_sums = target_sums + jnp.dot(grad_half, a_src[part, :], preferred_element_type=F32)
                source_ref[:, part] += jnp.dot(b_dst_t[:extra], grad_half, preferred_element_type=F32)
            if ahead:
                scores[:, part] = jnp.dot(b_dst[...], a_src_t[:, part], preferred_element_type=F32)
                outer[:, part] = jnp.dot(b_pair[...], a_pair_t[:, part], preferred_element_type=F32)
        if behind:
            for slot in range(cols_ref.shape[0]):
                here = slice(slot * own, (slot + 1) * own)
                cols_ref[slot, :own, :] = col_sums[here].astype(BF16)
                wide = jnp.concatenate([target_sums[here], jnp.zeros((pair - own, LANES), F32)], axis=0)
                cols_ref[slot, own:, :] = jnp.transpose(wide)[:extra].astype(BF16)

    @pl.when(step == 0)
    def _():
        source_ref[...] = start_ref[...] if last else jnp.zeros_like(source_ref)
        work(True, False)

    @pl.when((step > 0) & (step < end))
    def _():
        work(True, True)

    @pl.when(step == end)
    def _():
        work(False, True)
        if last:
            fill = jnp.zeros((extra, pair - own), F32)
            for chunk in range(slots.shape[0]):
                part = source_ref[:, chunk * own : (chunk + 1) * own]
                slots[place_ref[10] ^ chunk] = jnp.concatenate([part, fill], axis=1)
            for slot, piece_ref in enumerate(piece_refs):
                piece_ref[:own, :] = mine_ref[slot]
                piece_ref[own:, :] = slots[2 * slot].astype(BF16)
                twin_ref[slot] = slots[2 * slot + 1].astype(BF16)


def tile_sums(place, kept, half, table, late, own, feat, extra, last, name):
    rows, pair = kept[0].shape
    cols = kept[4].shape[0] // 2
    mates = rows // own
    step = pick(cols, 2 * own, 4 * own)
    tiles = cols // step
    base = half * tiles

    def now(i):
        return jnp.minimum(i, tiles - 1) + base

    def then(i):
        return jnp.maximum(i - 1, 0)

    scratch = [pltpu.VMEM((step, rows), F32)] * 2
    kinds = []
    if last:
        kinds = [((own + extra, pair), BF16)] * (mates // 2) + [((mates // 2, extra, pair), BF16)]
        scratch += [pltpu.VMEM((mates, extra, pair), F32)]
    work = 1 << 20 if last else 2 * rows * cols * 1280
    return pl.pallas_call(
        functools.partial(tile_kernel, own, feat, last),
        grid=(tiles + 1,),
        in_specs=[
            SMEM,
            *[whole(x.shape) for x in kept[:4]],
            pl.BlockSpec((step, pair), lambda i: (now(i), 0)),
            pl.BlockSpec((step, LANES), lambda i: (now(i), 0)),
            pl.BlockSpec((LANES, step), lambda i: (0, then(i) + base)),
            *[whole(x.shape) for x in (table, *late)],
        ],
        out_specs=[pl.BlockSpec((step // own, own + extra, pair), lambda i: (then(i), 0, 0)), whole((extra, rows))]
        + [whole(shape) for shape, kind in kinds],
        out_shape=shapes(((cols // own, own + extra, pair), BF16), ((extra, rows), F32), *kinds),
        scratch_shapes=scratch,
        compiler_params=params(),
        cost_estimate=pl.CostEstimate(flops=work, bytes_accessed=1 << 20, transcendentals=work >> 11),
        name=name,
    )(place, *kept, table, *late)


def join_cols_kernel(own_ref, other_ref, unused_ref, out_ref):
    out_ref[...] = (own_ref[...].astype(F32) + other_ref[...].astype(F32)).astype(BF16)


def join_rows_kernel(given_ref, twin_ref, *rest):
    count, own = given_ref.shape[:2]
    for slot, (piece_ref, out_ref) in enumerate(zip(rest[:count], rest[count + 1 :])):
        out_ref[:own, :] = (piece_ref[:own, :].astype(F32) + given_ref[slot].astype(F32)).astype(BF16)
        out_ref[own:, :] = (piece_ref[own:, :].astype(F32) + twin_ref[slot].astype(F32)).astype(BF16)


def join(kernel, name, outs, *arrays, unread=()):
    vmem, anywhere = pl.BlockSpec(memory_space=pltpu.VMEM), pl.BlockSpec(memory_space=pl.ANY)
    return pl.pallas_call(
        kernel,
        in_specs=[vmem] * len(arrays) + [anywhere] * len(unread),
        out_shape=[jax.ShapeDtypeStruct(out.shape, out.dtype) for out in outs],
        compiler_params=params(8),
        name=name,
    )(*arrays, *unread)


def finish_kernel(own, feat, emb_count, cols_ref, *rest):
    piece_refs, (hop_ref, grad_ref, source_ref, target_ref) = rest[:-4], rest[-4:]
    total = jnp.zeros((own, 2 * feat), F32)
    extra = jnp.zeros((cols_ref.shape[1] - own, 2 * feat), F32)
    source = extra
    for piece_ref in piece_refs:
        total = total + piece_ref[:own, :].astype(F32)
        source = source + piece_ref[own:, :].astype(F32)
    for slot in range(cols_ref.shape[0]):
        total = total + cols_ref[slot, :own, :].astype(F32)
        extra = extra + cols_ref[slot, own:, :].astype(F32)
    hop_ref[...] = total[:, :feat].astype(BF16)
    grad_ref[...] = total[:, feat:].astype(BF16)
    source_ref[...] = source[:emb_count, :own]
    target_ref[...] = extra[:emb_count, :own]


def finish(cols, pieces, own, feat, emb_count):
    return pl.pallas_call(
        functools.partial(finish_kernel, own, feat, emb_count),
        out_shape=shapes(
            ((own, feat), BF16), ((own, feat), BF16), ((emb_count, own), F32), ((emb_count, own), F32)
        ),
        compiler_params=params(8),
        name="finish",
    )(cols, *pieces)


def local(sizes, source_embed, target_embed, features, cotangent):
    row_size, col_size = sizes
    emb_count, own = source_embed.shape
    feat = features.shape[1]
    pair = 2 * feat
    extra = -(-emb_count // 16) * 16
    depth, width = row_size // 4, col_size // 2
    both = ("row", "col")

    def device(z, y, core, x, skew):
        return (((z % depth) * 2 + y) * 2 + core) * col_size + (x % width) * 2 + (skew ^ y)

    groups = [
        [device(z, y, core, x, skew) for z in range(depth) for y in range(2)]
        for core in range(2) for x in range(width) for skew in range(2)
    ]

    def mate(array, bits):
        return lax.ppermute(array, "col", [(c, c ^ bits) for c in range(col_size)])

    def swap(array):
        return lax.ppermute(array, "row", [(r, r ^ 1) for r in range(row_size)])

    def along_x(array, move, flip):
        pairs = [(x * 2 + y, ((x + move) % width) * 2 + (y ^ flip)) for x in range(width) for y in range(2)]
        return lax.ppermute(array, "col", pairs)

    def along_z(array, move, flip):
        pairs = [
            (device(z, y, core, x, skew), device(z + move, y ^ flip, core, x, skew))
            for z in range(depth) for y in range(2) for core in range(2) for x in range(width) for skew in range(2)
        ]
        return lax.ppermute(array, both, pairs)

    def pack(embed):
        left = jnp.pad(features, ((0, extra), (0, feat)))
        right = jnp.pad(cotangent, ((0, extra), (feat, 0)))
        return left + right + jnp.pad(embed, ((own, extra - emb_count), (0, pair - own)))

    index = lax.axis_index(both)
    place = lax.dynamic_index_in_dim(jnp.asarray(places(row_size, col_size)), index, 0, keepdims=False)
    chunks, alongs = (pack(target_embed), pack(source_embed)), (along_z, along_x)
    near = [jnp.stack([chunk, along(chunk, 0, 1)]) for chunk, along in zip(chunks, alongs)]
    near, place = lax.optimization_barrier((near, place))
    moved = [[along(array, -move, 0) for array, along in zip(near, alongs)] for move in MOVES[1:]]
    b_parts, a_parts = [[array, *[pair[index] for pair in moved]] for index, array in enumerate(near)]
    others = [swap(part) for part in b_parts]
    scaled, stats, kept = row_stats(place, a_parts, b_parts, others, own, feat)
    stats = lax.all_to_all(stats, "col", 0, 0)

    sizes = (own, feat, extra)
    table, mine, given = weigh(place, stats, scaled, own)
    given = mate(given, 1)
    other_cols, start = tile_sums(place, kept, 1, table, (), *sizes, False, "other_tile")
    other_cols = swap(other_cols)
    own_cols, unused, *pieces, twin = tile_sums(place, kept, 0, table, (start, mine), *sizes, True, "own_tile")
    twin = mate(twin, 1)
    (cols,) = join(join_cols_kernel, "join_cols", [own_cols], own_cols, other_cols, unread=(given,))
    pieces = join(join_rows_kernel, "join_rows", pieces, given, twin, *pieces, unread=(cols,))
    cols = lax.all_to_all(cols, both, 0, 0, axis_index_groups=groups)
    pieces = [mate(piece, 2 * slot) if slot else piece for slot, piece in enumerate(pieces)]
    return tuple(finish(cols, pieces, own, feat, emb_count))


def solution(mesh):
    nodes = P(("row", "col"), None)
    embeds = P(None, ("row", "col"))
    sizes = (mesh.shape["row"], mesh.shape["col"])
    return jax.shard_map(
        functools.partial(local, sizes),
        mesh=mesh,
        in_specs=(embeds, embeds, nodes, nodes),
        out_specs=(nodes, nodes, embeds, embeds),
        check_vma=False,
    )
```

```python
import functools

import jax
import jax.numpy as jnp
import numpy as np
from jax import lax
from jax.experimental import pallas as pl
from jax.experimental.pallas import tpu as pltpu
from jax.sharding import PartitionSpec as P

F32 = jnp.float32
BF16 = jnp.bfloat16
LANES = 128
VMEM_MIB = 24
SMEM = pl.BlockSpec(memory_space=pltpu.SMEM)
MOVES = (0, 1, 2, -1)


def pick(total, unit, most):
    size = total
    while size > most or total % size or size % unit:
        size -= unit
    return size


def whole(shape):
    return pl.BlockSpec(shape, lambda *i: (0,) * len(shape))


def shapes(*pairs):
    return [jax.ShapeDtypeStruct(shape, kind) for shape, kind in pairs]


def params(mib=VMEM_MIB):
    return pltpu.CompilerParams(vmem_limit_bytes=mib * 1024 * 1024)


def places(row_size, col_size):
    depth, width = row_size // 4, col_size // 2
    table = np.zeros((row_size * col_size, 16), np.int32)
    for index in range(row_size * col_size):
        row, col = divmod(index, col_size)
        slots = [(col // 2 + move) % width for move in MOVES] + [(row // 4 + move) % depth for move in MOVES]
        table[index, :12] = slots + [col % 2, row // 2 % 2, col, col // 2]
    return table


def assemble(own, chunk_refs, place_ref, base, parity, pair_ref, turned_ref, nodes_ref):
    extra = chunk_refs[0].shape[1] - own
    even = parity == 0
    blank = jnp.zeros((extra, 2 * own - chunk_refs[0].shape[2]), F32)
    for slot, chunk_ref in enumerate(chunk_refs):
        start = place_ref[base + slot] * 2 * own
        for flip in range(2):
            rows = pl.ds(pl.multiple_of(start + (parity ^ flip) * own, 64), own)
            pair_ref[rows, :] = chunk_ref[flip, :own, :]
        first = chunk_ref[0, own:, :].astype(F32)
        second = chunk_ref[1, own:, :].astype(F32)
        left = jnp.concatenate([jnp.where(even, first, second), blank], axis=1)
        right = jnp.concatenate([blank, jnp.where(even, second, first)], axis=1)
        both = left + pltpu.roll(right, own - blank.shape[1], 1)
        turned_ref[:extra, pl.ds(pl.multiple_of(start, LANES), 2 * own)] = both.astype(BF16)
    turned_ref[extra:, :] = jnp.zeros((LANES - extra, turned_ref.shape[1]), BF16)
    nodes_ref[...] = jnp.transpose(turned_ref[...])


def stats_kernel(own, feat, place_ref, *rest):
    parts = len(MOVES)
    a_refs, b0_refs, b1_refs = rest[0 : 2 * parts : 2], rest[1 : 2 * parts : 2], rest[2 * parts : 3 * parts]
    scaled_ref, stats_ref, a_pair, a_pair_t, a_src, a_src_t, b_pair, b_dst, b_dst_t, scores, peaks = rest[3 * parts :]
    step = pl.program_id(0)
    last = pl.num_programs(0) - 1
    count, cols = scores.shape
    span = pick(cols, LANES, 512)
    repeat = span // LANES

    def tiles(array):
        return [array[:, lane : lane + LANES] for lane in range(0, span, LANES)]

    def work(ahead, behind):
        block = step - 1 if behind else step
        here = pl.ds(pl.multiple_of(block * count, count), count)
        there = pl.ds(pl.multiple_of(step * count, count), count)
        total = jnp.zeros((count, LANES), F32)
        peak = jnp.zeros((count, LANES), F32)
        sums = jnp.zeros((count, 2 * feat), F32)
        for start in range(0, cols, span):
            part = slice(start, start + span)
            if behind:
                before = peaks[...]
                half = jnp.exp(scores[:, part] - jnp.concatenate([before] * repeat, axis=1)).astype(BF16)
                total = total + sum(tiles(half.astype(F32)))
                sums = sums + jnp.dot(half, b_pair[part, :], preferred_element_type=F32)
            if ahead:
                fresh = jnp.maximum(jnp.dot(a_src[there, :], b_dst_t[:, part], preferred_element_type=F32), 0.0)
                scores[:, part] = fresh
                peak = functools.reduce(jnp.maximum, tiles(fresh), peak)
        if behind:
            total = jnp.sum(total, axis=1, keepdims=True)
            sums = sums / total
            scaled_ref[...] = sums.astype(BF16)
            mates = a_pair[here, :].astype(F32)
            inner = jnp.sum(sums[:, :feat] * mates[:, feat:] + sums[:, feat:] * mates[:, :feat], axis=1, keepdims=True)
            lane = lax.broadcasted_iota(jnp.int32, (count, LANES), 1)
            table = jnp.where(lane == 0, peaks[...], jnp.where(lane == 1, total, inner))
            stats_ref[...] = jnp.broadcast_to(jnp.transpose(table)[:4][None], stats_ref.shape)
        if ahead:
            peaks[...] = jnp.broadcast_to(jnp.max(peak, axis=1, keepdims=True), peaks.shape)

    @pl.when(step == 0)
    def _():
        assemble(own, a_refs, place_ref, 0, place_ref[8], a_pair, a_src_t, a_src)
        half = b_pair.shape[0] // 2
        for index, b_refs in enumerate((b0_refs, b1_refs)):
            part = pl.ds(index * half, half)
            outs = (b_pair.at[part, :], b_dst_t.at[:, part], b_dst.at[part, :])
            assemble(own, b_refs, place_ref, 4, place_ref[9], *outs)
        a_pair_t[:feat] = jnp.transpose(a_pair[:, feat:])
        a_pair_t[feat:] = jnp.transpose(a_pair[:, :feat])
        work(True, False)

    @pl.when((step > 0) & (step < last))
    def _():
        work(True, True)

    @pl.when(step == last)
    def _():
        work(False, True)


def row_stats(place, a_parts, b0_parts, b1_parts, own, feat):
    mates = sum(part.shape[0] for part in a_parts)
    rows = mates * own
    cols = 2 * own * sum(part.shape[0] for part in b0_parts)
    pair = 2 * feat
    step = pick(rows, LANES, 512)
    kept = [((rows, pair), BF16), ((pair, rows), BF16), ((rows, LANES), BF16), ((LANES, rows), BF16)]
    kept += [((cols, pair), BF16), ((cols, LANES), BF16), ((LANES, cols), BF16)]
    parts = [part for both in zip(a_parts, b0_parts) for part in both] + b1_parts
    scaled, stats, *kept = pl.pallas_call(
        functools.partial(stats_kernel, own, feat),
        grid=(rows // step + 1,),
        in_specs=[SMEM] + [whole(x.shape) for x in parts],
        out_specs=[
            pl.BlockSpec((step, pair), lambda i: (jnp.maximum(i - 1, 0), 0)),
            pl.BlockSpec((mates, 4, step), lambda i: (0, 0, jnp.maximum(i - 1, 0))),
        ]
        + [whole(shape) for shape, kind in kept],
        out_shape=shapes(((rows, pair), BF16), ((mates, 4, rows), F32), *kept),
        scratch_shapes=[pltpu.VMEM((step, cols), F32), pltpu.VMEM((step, LANES), F32)],
        compiler_params=params(),
        cost_estimate=pl.CostEstimate(flops=2 * rows * cols * 512, bytes_accessed=8 << 20, transcendentals=rows * cols),
        name="row_stats",
    )(place, *parts)
    return scaled, stats, kept


def weigh_kernel(own, place_ref, stats_ref, scaled_ref, table_ref, mine_ref, given_ref, weights_ref):
    stats = stats_ref[...]
    peaks = stats[:, 0:1]
    peak = jnp.max(peaks, axis=0)
    weights = jnp.exp(peaks - peak[None]) * stats[:, 1:2]
    total = jnp.sum(weights, axis=0)
    table_ref[0:1, :] = peak + jnp.log(total)
    table_ref[1:2, :] = jnp.sum(weights * stats[:, 2:3], axis=0) / total
    table_ref[2:, :] = jnp.zeros((table_ref.shape[0] - 2, table_ref.shape[1]), F32)
    at = place_ref[10]
    weight = jnp.exp(stats_ref[at, 0:1] - peak) * stats_ref[at, 1:2] / total
    weights_ref[...] = jnp.transpose(jnp.broadcast_to(weight, (LANES, weight.shape[1])))
    for slot in range(mine_ref.shape[0]):
        for flip, out_ref in enumerate((mine_ref, given_ref)):
            chunk = 2 * (place_ref[11] ^ slot) + (place_ref[8] ^ flip)
            rows = pl.ds(pl.multiple_of(chunk * own, 64), own)
            out_ref[slot] = (weights_ref[rows, 0:1] * scaled_ref[rows, :].astype(F32)).astype(BF16)


def weigh(place, stats, scaled, own):
    rows, pair = scaled.shape
    count = stats.shape[0] // 2
    part = ((count, own, pair), BF16)
    return pl.pallas_call(
        functools.partial(weigh_kernel, own),
        in_specs=[SMEM] + [pl.BlockSpec(memory_space=pltpu.VMEM)] * 2,
        out_shape=shapes(((8, rows), F32), part, part),
        scratch_shapes=[pltpu.VMEM((rows, LANES), F32)],
        compiler_params=params(8),
        name="weigh",
    )(place, stats, scaled)


def tile_kernel(own, feat, half, place_ref, a_pair, a_pair_t, a_src, a_src_t, b_pair, b_dst, b_dst_t, table, *rest):
    pair = 2 * feat
    last = half == 0
    if last:
        start_ref, mine_ref, cols_ref, source_ref, *piece_refs, twin_ref = rest[:-5]
        col_sums, target_sums, scores, outer, slots = rest[-5:]
    else:
        cols_ref, source_ref, col_sums, target_sums, scores, outer = rest
    extra = cols_ref.shape[1] - own
    rows = a_pair.shape[0]
    cols = col_sums.shape[0]
    span = scores.shape[2]
    here = slice(half * cols, (half + 1) * cols)

    def ahead(index):
        part = slice(index * span, (index + 1) * span)
        scores[index % 2] = jnp.dot(b_dst[here, :], a_src_t[:, part], preferred_element_type=F32)
        outer[index % 2] = jnp.dot(b_pair[here, :], a_pair_t[:, part], preferred_element_type=F32)

    def behind(index):
        part = slice(index * span, (index + 1) * span)
        score = scores[index % 2]
        soft = jnp.exp(jnp.maximum(score, 0.0) - table[0:1, part])
        grad = jnp.where(score > 0.0, soft * (outer[index % 2] - table[1:2, part]), 0.0)
        soft_half = soft.astype(BF16)
        grad_half = grad.astype(BF16)
        more_cols = jnp.dot(soft_half, a_pair[part, :], preferred_element_type=F32)
        more_target = jnp.dot(grad_half, a_src[part, :], preferred_element_type=F32)
        more_source = jnp.dot(b_dst_t[:extra, here], grad_half, preferred_element_type=F32)
        col_sums[...] = col_sums[...] + more_cols if index else more_cols
        target_sums[...] = target_sums[...] + more_target if index else more_target
        source_ref[:, part] = start_ref[:, part] + more_source if last else more_source

    count = rows // span
    ahead(0)
    for index in range(count):
        if index + 1 < count:
            ahead(index + 1)
        behind(index)
    for slot in range(cols_ref.shape[0]):
        chunk = slice(slot * own, (slot + 1) * own)
        cols_ref[slot, :own, :] = col_sums[chunk, :].astype(BF16)
        wide = jnp.concatenate([target_sums[chunk, :], jnp.zeros((pair - own, LANES), F32)], axis=0)
        cols_ref[slot, own:, :] = jnp.transpose(wide)[:extra].astype(BF16)
    if last:
        fill = jnp.zeros((extra, pair - own), F32)
        for chunk in range(slots.shape[0]):
            part = source_ref[:, chunk * own : (chunk + 1) * own]
            slots[place_ref[10] ^ chunk] = jnp.concatenate([part, fill], axis=1)
        for slot, piece_ref in enumerate(piece_refs):
            piece_ref[:own, :] = mine_ref[slot]
            piece_ref[own:, :] = slots[2 * slot].astype(BF16)
            twin_ref[slot] = slots[2 * slot + 1].astype(BF16)


def tile_sums(place, kept, half, table, late, unread, own, feat, extra, name):
    rows, pair = kept[0].shape
    cols = kept[4].shape[0] // 2
    mates = rows // own
    span = pick(rows, LANES, 256)
    scratch = [pltpu.VMEM((cols, pair), F32), pltpu.VMEM((cols, LANES), F32)] + [pltpu.VMEM((2, cols, span), F32)] * 2
    kinds = []
    if half == 0:
        kinds = [((own + extra, pair), BF16)] * (mates // 2) + [((mates // 2, extra, pair), BF16)]
        scratch += [pltpu.VMEM((mates, extra, pair), F32)]
    vmem, anywhere = pl.BlockSpec(memory_space=pltpu.VMEM), pl.BlockSpec(memory_space=pl.ANY)
    work = 1 << 20 if half == 0 else 2 * rows * cols * 1280
    return pl.pallas_call(
        functools.partial(tile_kernel, own, feat, half),
        in_specs=[SMEM] + [vmem] * (len(kept) + 1 + len(late)) + [anywhere] * len(unread),
        out_shape=shapes(((cols // own, own + extra, pair), BF16), ((extra, rows), F32), *kinds),
        scratch_shapes=scratch,
        compiler_params=params(),
        cost_estimate=pl.CostEstimate(flops=work, bytes_accessed=1 << 20, transcendentals=work >> 11),
        name=name,
    )(place, *kept, table, *late, *unread)


def join_cols_kernel(own_ref, other_ref, unread_ref, out_ref):
    out_ref[...] = (own_ref[...].astype(F32) + other_ref[...].astype(F32)).astype(BF16)


def join_rows_kernel(given_ref, twin_ref, *rest):
    count, own = given_ref.shape[:2]
    for slot, (piece_ref, out_ref) in enumerate(zip(rest[:count], rest[count + 1 :])):
        out_ref[:own, :] = (piece_ref[:own, :].astype(F32) + given_ref[slot].astype(F32)).astype(BF16)
        out_ref[own:, :] = (piece_ref[own:, :].astype(F32) + twin_ref[slot].astype(F32)).astype(BF16)


def join(kernel, name, outs, *arrays, unread=()):
    vmem, anywhere = pl.BlockSpec(memory_space=pltpu.VMEM), pl.BlockSpec(memory_space=pl.ANY)
    return pl.pallas_call(
        kernel,
        in_specs=[vmem] * len(arrays) + [anywhere] * len(unread),
        out_shape=[jax.ShapeDtypeStruct(out.shape, out.dtype) for out in outs],
        compiler_params=params(8),
        name=name,
    )(*arrays, *unread)


def finish_kernel(own, feat, emb_count, cols_ref, *rest):
    piece_refs, (hop_ref, grad_ref, source_ref, target_ref) = rest[:-4], rest[-4:]
    total = jnp.zeros((own, 2 * feat), F32)
    extra = jnp.zeros((cols_ref.shape[1] - own, 2 * feat), F32)
    source = extra
    for piece_ref in piece_refs:
        total = total + piece_ref[:own, :].astype(F32)
        source = source + piece_ref[own:, :].astype(F32)
    for slot in range(cols_ref.shape[0]):
        total = total + cols_ref[slot, :own, :].astype(F32)
        extra = extra + cols_ref[slot, own:, :].astype(F32)
    hop_ref[...] = total[:, :feat].astype(BF16)
    grad_ref[...] = total[:, feat:].astype(BF16)
    source_ref[...] = source[:emb_count, :own]
    target_ref[...] = extra[:emb_count, :own]


def finish(cols, pieces, own, feat, emb_count):
    return pl.pallas_call(
        functools.partial(finish_kernel, own, feat, emb_count),
        out_shape=shapes(
            ((own, feat), BF16), ((own, feat), BF16), ((emb_count, own), F32), ((emb_count, own), F32)
        ),
        compiler_params=params(8),
        name="finish",
    )(cols, *pieces)


def local(sizes, source_embed, target_embed, features, cotangent):
    row_size, col_size = sizes
    emb_count, own = source_embed.shape
    feat = features.shape[1]
    pair = 2 * feat
    extra = -(-emb_count // 16) * 16
    depth, width = row_size // 4, col_size // 2
    both = ("row", "col")

    def device(z, y, core, x, skew):
        return (((z % depth) * 2 + y) * 2 + core) * col_size + (x % width) * 2 + (skew ^ y)

    groups = [
        [device(z, y, core, x, skew) for z in range(depth) for y in range(2)]
        for core in range(2) for x in range(width) for skew in range(2)
    ]

    def mate(array, bits):
        return lax.ppermute(array, "col", [(c, c ^ bits) for c in range(col_size)])

    def swap(array):
        return lax.ppermute(array, "row", [(r, r ^ 1) for r in range(row_size)])

    def along_x(array, move, flip):
        pairs = [(x * 2 + y, ((x + move) % width) * 2 + (y ^ flip)) for x in range(width) for y in range(2)]
        return lax.ppermute(array, "col", pairs)

    def along_z(array, move, flip):
        pairs = [
            (device(z, y, core, x, skew), device(z + move, y ^ flip, core, x, skew))
            for z in range(depth) for y in range(2) for core in range(2) for x in range(width) for skew in range(2)
        ]
        return lax.ppermute(array, both, pairs)

    def pack(embed):
        left = jnp.pad(features, ((0, extra), (0, feat)))
        right = jnp.pad(cotangent, ((0, extra), (feat, 0)))
        return left + right + jnp.pad(embed, ((own, extra - emb_count), (0, pair - own)))

    index = lax.axis_index(both)
    place = lax.dynamic_index_in_dim(jnp.asarray(places(row_size, col_size)), index, 0, keepdims=False)
    chunks, alongs = (pack(target_embed), pack(source_embed)), (along_z, along_x)
    near = [jnp.stack([chunk, along(chunk, 0, 1)]) for chunk, along in zip(chunks, alongs)]
    near, place = lax.optimization_barrier((near, place))
    moved = [[along(array, -move, 0) for array, along in zip(near, alongs)] for move in MOVES[1:]]
    b_parts, a_parts = [[array, *[pair[index] for pair in moved]] for index, array in enumerate(near)]
    others = [swap(part) for part in b_parts]
    scaled, stats, kept = row_stats(place, a_parts, b_parts, others, own, feat)
    stats = lax.all_to_all(stats, "col", 0, 0)

    sizes = (own, feat, extra)
    table, mine, *given = weigh(place, stats, scaled, own)
    given = [mate(part, 1) for part in given]
    other_cols, start = tile_sums(place, kept, 1, table, (), (), *sizes, "other_tile")
    other_cols = swap(other_cols)
    own_cols, unused, *pieces, twin = tile_sums(place, kept, 0, table, (start, mine), (), *sizes, "own_tile")
    twin = mate(twin, 1)
    (cols,) = join(join_cols_kernel, "join_cols", [own_cols], own_cols, other_cols, unread=given)
    pieces = join(join_rows_kernel, "join_rows", pieces, *given, twin, *pieces, unread=(cols,))
    cols = lax.all_to_all(cols, both, 0, 0, axis_index_groups=groups)
    pieces = [mate(piece, 2 * slot) if slot else piece for slot, piece in enumerate(pieces)]
    return tuple(finish(cols, pieces, own, feat, emb_count))


def solution(mesh):
    nodes = P(("row", "col"), None)
    embeds = P(None, ("row", "col"))
    sizes = (mesh.shape["row"], mesh.shape["col"])
    return jax.shard_map(
        functools.partial(local, sizes),
        mesh=mesh,
        in_specs=(embeds, embeds, nodes, nodes),
        out_specs=(nodes, nodes, embeds, embeds),
        check_vma=False,
    )
```

```python
import functools

import jax
import jax.numpy as jnp
import numpy as np
from jax import lax
from jax.experimental import pallas as pl
from jax.experimental.pallas import tpu as pltpu
from jax.sharding import PartitionSpec as P

F32 = jnp.float32
BF16 = jnp.bfloat16
LANES = 128
VMEM_MIB = 24
SMEM = pl.BlockSpec(memory_space=pltpu.SMEM)
MOVES = (0, 1, 2, -1)


def pick(total, unit, most):
    size = total
    while size > most or total % size or size % unit:
        size -= unit
    return size


def whole(shape):
    return pl.BlockSpec(shape, lambda *i: (0,) * len(shape))


def shapes(*pairs):
    return [jax.ShapeDtypeStruct(shape, kind) for shape, kind in pairs]


def params(mib=VMEM_MIB):
    return pltpu.CompilerParams(vmem_limit_bytes=mib * 1024 * 1024)


def places(row_size, col_size):
    depth, width = row_size // 4, col_size // 2
    table = np.zeros((row_size * col_size, 16), np.int32)
    for index in range(row_size * col_size):
        row, col = divmod(index, col_size)
        slots = [(col // 2 + move) % width for move in MOVES] + [(row // 4 + move) % depth for move in MOVES]
        table[index, :12] = slots + [col % 2, row // 2 % 2, col, col // 2]
    return table


def assemble(own, chunk_refs, place_ref, base, parity, pair_ref, turned_ref, nodes_ref):
    extra = chunk_refs[0].shape[1] - own
    even = parity == 0
    blank = jnp.zeros((extra, 2 * own - chunk_refs[0].shape[2]), F32)
    for slot, chunk_ref in enumerate(chunk_refs):
        start = place_ref[base + slot] * 2 * own
        for flip in range(2):
            rows = pl.ds(pl.multiple_of(start + (parity ^ flip) * own, 64), own)
            pair_ref[rows, :] = chunk_ref[flip, :own, :]
        first = chunk_ref[0, own:, :].astype(F32)
        second = chunk_ref[1, own:, :].astype(F32)
        left = jnp.concatenate([jnp.where(even, first, second), blank], axis=1)
        right = jnp.concatenate([blank, jnp.where(even, second, first)], axis=1)
        both = left + pltpu.roll(right, own - blank.shape[1], 1)
        turned_ref[:extra, pl.ds(pl.multiple_of(start, LANES), 2 * own)] = both.astype(BF16)
    turned_ref[extra:, :] = jnp.zeros((LANES - extra, turned_ref.shape[1]), BF16)
    nodes_ref[...] = jnp.transpose(turned_ref[...])


def rows_kernel(own, feat, place_ref, *rest):
    a_refs, (a_pair, a_pair_t, a_src, a_src_t) = rest[: len(MOVES)], rest[len(MOVES) :]
    assemble(own, a_refs, place_ref, 0, place_ref[8], a_pair, a_src_t, a_src)
    a_pair_t[:feat] = jnp.transpose(a_pair[:, feat:])
    a_pair_t[feat:] = jnp.transpose(a_pair[:, :feat])


def row_arrays(place, a_parts, own, feat):
    rows = own * sum(part.shape[0] for part in a_parts)
    pair = 2 * feat
    return pl.pallas_call(
        functools.partial(rows_kernel, own, feat),
        in_specs=[SMEM] + [pl.BlockSpec(memory_space=pltpu.VMEM)] * len(a_parts),
        out_shape=shapes(((rows, pair), BF16), ((pair, rows), BF16), ((rows, LANES), BF16), ((LANES, rows), BF16)),
        compiler_params=params(8),
        cost_estimate=pl.CostEstimate(flops=1 << 30, bytes_accessed=1 << 20, transcendentals=0),
        name="row_arrays",
    )(place, *a_parts)


def stats_kernel(own, feat, place_ref, a_pair, a_src, *rest):
    parts = len(MOVES)
    b0_refs, b1_refs = rest[:parts], rest[parts : 2 * parts]
    scaled_ref, stats_ref, b_pair, b_dst, b_dst_t, scores, peaks = rest[2 * parts :]
    step = pl.program_id(0)
    last = pl.num_programs(0) - 1
    count, cols = scores.shape
    span = pick(cols, LANES, 512)
    repeat = span // LANES

    def tiles(array):
        return [array[:, lane : lane + LANES] for lane in range(0, span, LANES)]

    def work(ahead, behind):
        block = step - 1 if behind else step
        here = pl.ds(pl.multiple_of(block * count, count), count)
        there = pl.ds(pl.multiple_of(step * count, count), count)
        total = jnp.zeros((count, LANES), F32)
        peak = jnp.zeros((count, LANES), F32)
        sums = jnp.zeros((count, 2 * feat), F32)
        for start in range(0, cols, span):
            part = slice(start, start + span)
            if behind:
                before = peaks[...]
                half = jnp.exp(scores[:, part] - jnp.concatenate([before] * repeat, axis=1)).astype(BF16)
                total = total + sum(tiles(half.astype(F32)))
                sums = sums + jnp.dot(half, b_pair[part, :], preferred_element_type=F32)
            if ahead:
                fresh = jnp.maximum(jnp.dot(a_src[there, :], b_dst_t[:, part], preferred_element_type=F32), 0.0)
                scores[:, part] = fresh
                peak = functools.reduce(jnp.maximum, tiles(fresh), peak)
        if behind:
            total = jnp.sum(total, axis=1, keepdims=True)
            sums = sums / total
            scaled_ref[...] = sums.astype(BF16)
            mates = a_pair[here, :].astype(F32)
            inner = jnp.sum(sums[:, :feat] * mates[:, feat:] + sums[:, feat:] * mates[:, :feat], axis=1, keepdims=True)
            lane = lax.broadcasted_iota(jnp.int32, (count, LANES), 1)
            table = jnp.where(lane == 0, peaks[...], jnp.where(lane == 1, total, inner))
            stats_ref[...] = jnp.broadcast_to(jnp.transpose(table)[:4][None], stats_ref.shape)
        if ahead:
            peaks[...] = jnp.broadcast_to(jnp.max(peak, axis=1, keepdims=True), peaks.shape)

    @pl.when(step == 0)
    def _():
        half = b_pair.shape[0] // 2
        for index, b_refs in enumerate((b0_refs, b1_refs)):
            part = pl.ds(index * half, half)
            outs = (b_pair.at[part, :], b_dst_t.at[:, part], b_dst.at[part, :])
            assemble(own, b_refs, place_ref, 4, place_ref[9], *outs)
        work(True, False)

    @pl.when((step > 0) & (step < last))
    def _():
        work(True, True)

    @pl.when(step == last)
    def _():
        work(False, True)


def row_stats(place, a_kept, b0_parts, b1_parts, own, feat):
    rows = a_kept[0].shape[0]
    mates = rows // own
    cols = 2 * own * sum(part.shape[0] for part in b0_parts)
    pair = 2 * feat
    step = pick(rows, LANES, 512)
    kept = [((cols, pair), BF16), ((cols, LANES), BF16), ((LANES, cols), BF16)]
    parts = (a_kept[0], a_kept[2], *b0_parts, *b1_parts)
    scaled, stats, *kept = pl.pallas_call(
        functools.partial(stats_kernel, own, feat),
        grid=(rows // step + 1,),
        in_specs=[SMEM] + [whole(x.shape) for x in parts],
        out_specs=[
            pl.BlockSpec((step, pair), lambda i: (jnp.maximum(i - 1, 0), 0)),
            pl.BlockSpec((mates, 4, step), lambda i: (0, 0, jnp.maximum(i - 1, 0))),
        ]
        + [whole(shape) for shape, kind in kept],
        out_shape=shapes(((rows, pair), BF16), ((mates, 4, rows), F32), *kept),
        scratch_shapes=[pltpu.VMEM((step, cols), F32), pltpu.VMEM((step, LANES), F32)],
        compiler_params=params(),
        cost_estimate=pl.CostEstimate(flops=2 * rows * cols * 512, bytes_accessed=8 << 20, transcendentals=rows * cols),
        name="row_stats",
    )(place, *parts)
    return scaled, stats, [*a_kept, *kept]


def weigh_kernel(own, place_ref, stats_ref, scaled_ref, table_ref, mine_ref, given_ref, weights_ref):
    stats = stats_ref[...]
    peaks = stats[:, 0:1]
    peak = jnp.max(peaks, axis=0)
    weights = jnp.exp(peaks - peak[None]) * stats[:, 1:2]
    total = jnp.sum(weights, axis=0)
    table_ref[0:1, :] = peak + jnp.log(total)
    table_ref[1:2, :] = jnp.sum(weights * stats[:, 2:3], axis=0) / total
    table_ref[2:, :] = jnp.zeros((table_ref.shape[0] - 2, table_ref.shape[1]), F32)
    at = place_ref[10]
    weight = jnp.exp(stats_ref[at, 0:1] - peak) * stats_ref[at, 1:2] / total
    weights_ref[...] = jnp.transpose(jnp.broadcast_to(weight, (LANES, weight.shape[1])))
    for slot in range(mine_ref.shape[0]):
        for flip, out_ref in enumerate((mine_ref, given_ref)):
            chunk = 2 * (place_ref[11] ^ slot) + (place_ref[8] ^ flip)
            rows = pl.ds(pl.multiple_of(chunk * own, 64), own)
            out_ref[slot] = (weights_ref[rows, 0:1] * scaled_ref[rows, :].astype(F32)).astype(BF16)


def weigh(place, stats, scaled, own):
    rows, pair = scaled.shape
    count = stats.shape[0] // 2
    part = ((count, own, pair), BF16)
    return pl.pallas_call(
        functools.partial(weigh_kernel, own),
        in_specs=[SMEM] + [pl.BlockSpec(memory_space=pltpu.VMEM)] * 2,
        out_shape=shapes(((8, rows), F32), part, part),
        scratch_shapes=[pltpu.VMEM((rows, LANES), F32)],
        compiler_params=params(8),
        name="weigh",
    )(place, stats, scaled)


def tile_kernel(own, feat, half, place_ref, a_pair, a_pair_t, a_src, a_src_t, b_pair, b_dst, b_dst_t, table, *rest):
    pair = 2 * feat
    last = half == 0
    if last:
        start_ref, mine_ref, cols_ref, source_ref, *piece_refs, twin_ref = rest[:-5]
        col_sums, target_sums, scores, outer, slots = rest[-5:]
    else:
        cols_ref, source_ref, col_sums, target_sums, scores, outer = rest
    extra = cols_ref.shape[1] - own
    rows = a_pair.shape[0]
    cols = col_sums.shape[0]
    span = scores.shape[2]
    here = slice(half * cols, (half + 1) * cols)

    def ahead(index):
        part = slice(index * span, (index + 1) * span)
        scores[index % 2] = jnp.dot(b_dst[here, :], a_src_t[:, part], preferred_element_type=F32)
        outer[index % 2] = jnp.dot(b_pair[here, :], a_pair_t[:, part], preferred_element_type=F32)

    def behind(index):
        part = slice(index * span, (index + 1) * span)
        score = scores[index % 2]
        soft = jnp.exp(jnp.maximum(score, 0.0) - table[0:1, part])
        grad = jnp.where(score > 0.0, soft * (outer[index % 2] - table[1:2, part]), 0.0)
        soft_half = soft.astype(BF16)
        grad_half = grad.astype(BF16)
        more_cols = jnp.dot(soft_half, a_pair[part, :], preferred_element_type=F32)
        more_target = jnp.dot(grad_half, a_src[part, :], preferred_element_type=F32)
        more_source = jnp.dot(b_dst_t[:extra, here], grad_half, preferred_element_type=F32)
        col_sums[...] = col_sums[...] + more_cols if index else more_cols
        target_sums[...] = target_sums[...] + more_target if index else more_target
        source_ref[:, part] = start_ref[:, part] + more_source if last else more_source

    count = rows // span
    ahead(0)
    for index in range(count):
        if index + 1 < count:
            ahead(index + 1)
        behind(index)
    for slot in range(cols_ref.shape[0]):
        chunk = slice(slot * own, (slot + 1) * own)
        cols_ref[slot, :own, :] = col_sums[chunk, :].astype(BF16)
        wide = jnp.concatenate([target_sums[chunk, :], jnp.zeros((pair - own, LANES), F32)], axis=0)
        cols_ref[slot, own:, :] = jnp.transpose(wide)[:extra].astype(BF16)
    if last:
        fill = jnp.zeros((extra, pair - own), F32)
        for chunk in range(slots.shape[0]):
            part = source_ref[:, chunk * own : (chunk + 1) * own]
            slots[place_ref[10] ^ chunk] = jnp.concatenate([part, fill], axis=1)
        for slot, piece_ref in enumerate(piece_refs):
            piece_ref[:own, :] = mine_ref[slot]
            piece_ref[own:, :] = slots[2 * slot].astype(BF16)
            twin_ref[slot] = slots[2 * slot + 1].astype(BF16)


def tile_sums(place, kept, half, table, late, unread, own, feat, extra, name):
    rows, pair = kept[0].shape
    cols = kept[4].shape[0] // 2
    mates = rows // own
    span = pick(rows, LANES, 256)
    scratch = [pltpu.VMEM((cols, pair), F32), pltpu.VMEM((cols, LANES), F32)] + [pltpu.VMEM((2, cols, span), F32)] * 2
    kinds = []
    if half == 0:
        kinds = [((own + extra, pair), BF16)] * (mates // 2) + [((mates // 2, extra, pair), BF16)]
        scratch += [pltpu.VMEM((mates, extra, pair), F32)]
    vmem, anywhere = pl.BlockSpec(memory_space=pltpu.VMEM), pl.BlockSpec(memory_space=pl.ANY)
    work = 1 << 20 if half == 0 else 2 * rows * cols * 1280
    return pl.pallas_call(
        functools.partial(tile_kernel, own, feat, half),
        in_specs=[SMEM] + [vmem] * (len(kept) + 1 + len(late)) + [anywhere] * len(unread),
        out_shape=shapes(((cols // own, own + extra, pair), BF16), ((extra, rows), F32), *kinds),
        scratch_shapes=scratch,
        compiler_params=params(),
        cost_estimate=pl.CostEstimate(flops=work, bytes_accessed=1 << 20, transcendentals=work >> 11),
        name=name,
    )(place, *kept, table, *late, *unread)


def join_cols_kernel(own_ref, other_ref, unread_ref, out_ref):
    out_ref[...] = (own_ref[...].astype(F32) + other_ref[...].astype(F32)).astype(BF16)


def join_rows_kernel(given_ref, twin_ref, *rest):
    count, own = given_ref.shape[:2]
    for slot, (piece_ref, out_ref) in enumerate(zip(rest[:count], rest[count + 1 :])):
        out_ref[:own, :] = (piece_ref[:own, :].astype(F32) + given_ref[slot].astype(F32)).astype(BF16)
        out_ref[own:, :] = (piece_ref[own:, :].astype(F32) + twin_ref[slot].astype(F32)).astype(BF16)


def join(kernel, name, outs, *arrays, unread=()):
    vmem, anywhere = pl.BlockSpec(memory_space=pltpu.VMEM), pl.BlockSpec(memory_space=pl.ANY)
    return pl.pallas_call(
        kernel,
        in_specs=[vmem] * len(arrays) + [anywhere] * len(unread),
        out_shape=[jax.ShapeDtypeStruct(out.shape, out.dtype) for out in outs],
        compiler_params=params(8),
        name=name,
    )(*arrays, *unread)


def finish_kernel(own, feat, emb_count, cols_ref, *rest):
    piece_refs, (hop_ref, grad_ref, source_ref, target_ref) = rest[:-4], rest[-4:]
    total = jnp.zeros((own, 2 * feat), F32)
    extra = jnp.zeros((cols_ref.shape[1] - own, 2 * feat), F32)
    source = extra
    for piece_ref in piece_refs:
        total = total + piece_ref[:own, :].astype(F32)
        source = source + piece_ref[own:, :].astype(F32)
    for slot in range(cols_ref.shape[0]):
        total = total + cols_ref[slot, :own, :].astype(F32)
        extra = extra + cols_ref[slot, own:, :].astype(F32)
    hop_ref[...] = total[:, :feat].astype(BF16)
    grad_ref[...] = total[:, feat:].astype(BF16)
    source_ref[...] = source[:emb_count, :own]
    target_ref[...] = extra[:emb_count, :own]


def finish(cols, pieces, own, feat, emb_count):
    return pl.pallas_call(
        functools.partial(finish_kernel, own, feat, emb_count),
        out_shape=shapes(
            ((own, feat), BF16), ((own, feat), BF16), ((emb_count, own), F32), ((emb_count, own), F32)
        ),
        compiler_params=params(8),
        name="finish",
    )(cols, *pieces)


def local(sizes, source_embed, target_embed, features, cotangent):
    row_size, col_size = sizes
    emb_count, own = source_embed.shape
    feat = features.shape[1]
    pair = 2 * feat
    extra = -(-emb_count // 16) * 16
    depth, width = row_size // 4, col_size // 2
    both = ("row", "col")

    def device(z, y, core, x, skew):
        return (((z % depth) * 2 + y) * 2 + core) * col_size + (x % width) * 2 + (skew ^ y)

    groups = [
        [device(z, y, core, x, skew) for z in range(depth) for y in range(2)]
        for core in range(2) for x in range(width) for skew in range(2)
    ]

    def mate(array, bits):
        return lax.ppermute(array, "col", [(c, c ^ bits) for c in range(col_size)])

    def swap(array):
        return lax.ppermute(array, "row", [(r, r ^ 1) for r in range(row_size)])

    def along_x(array, move, flip):
        pairs = [(x * 2 + y, ((x + move) % width) * 2 + (y ^ flip)) for x in range(width) for y in range(2)]
        return lax.ppermute(array, "col", pairs)

    def along_z(array, move, flip):
        pairs = [
            (device(z, y, core, x, skew), device(z + move, y ^ flip, core, x, skew))
            for z in range(depth) for y in range(2) for core in range(2) for x in range(width) for skew in range(2)
        ]
        return lax.ppermute(array, both, pairs)

    def pack(embed):
        left = jnp.pad(features, ((0, extra), (0, feat)))
        right = jnp.pad(cotangent, ((0, extra), (feat, 0)))
        return left + right + jnp.pad(embed, ((own, extra - emb_count), (0, pair - own)))

    index = lax.axis_index(both)
    place = lax.dynamic_index_in_dim(jnp.asarray(places(row_size, col_size)), index, 0, keepdims=False)
    chunks, alongs = (pack(target_embed), pack(source_embed)), (along_z, along_x)
    near = [jnp.stack([chunk, along(chunk, 0, 1)]) for chunk, along in zip(chunks, alongs)]
    near, place = lax.optimization_barrier((near, place))
    moved = [[along(array, -move, 0) for array, along in zip(near, alongs)] for move in MOVES[1:]]
    b_parts, a_parts = [[array, *[pair[index] for pair in moved]] for index, array in enumerate(near)]
    others = [swap(part) for part in b_parts]
    a_kept = row_arrays(place, a_parts, own, feat)
    scaled, stats, kept = row_stats(place, a_kept, b_parts, others, own, feat)
    stats = lax.all_to_all(stats, "col", 0, 0)

    sizes = (own, feat, extra)
    table, mine, *given = weigh(place, stats, scaled, own)
    given = [mate(part, 1) for part in given]
    other_cols, start = tile_sums(place, kept, 1, table, (), (), *sizes, "other_tile")
    other_cols = swap(other_cols)
    own_cols, unused, *pieces, twin = tile_sums(place, kept, 0, table, (start, mine), (), *sizes, "own_tile")
    twin = mate(twin, 1)
    (cols,) = join(join_cols_kernel, "join_cols", [own_cols], own_cols, other_cols, unread=given)
    pieces = join(join_rows_kernel, "join_rows", pieces, *given, twin, *pieces, unread=(cols,))
    cols = lax.all_to_all(cols, both, 0, 0, axis_index_groups=groups)
    pieces = [mate(piece, 2 * slot) if slot else piece for slot, piece in enumerate(pieces)]
    return tuple(finish(cols, pieces, own, feat, emb_count))


def solution(mesh):
    nodes = P(("row", "col"), None)
    embeds = P(None, ("row", "col"))
    sizes = (mesh.shape["row"], mesh.shape["col"])
    return jax.shard_map(
        functools.partial(local, sizes),
        mesh=mesh,
        in_specs=(embeds, embeds, nodes, nodes),
        out_specs=(nodes, nodes, embeds, embeds),
        check_vma=False,
    )
```

```python
import functools

import jax
import jax.numpy as jnp
import numpy as np
from jax import lax
from jax.experimental import pallas as pl
from jax.experimental.pallas import tpu as pltpu
from jax.sharding import PartitionSpec as P

F32 = jnp.float32
BF16 = jnp.bfloat16
LANES = 128
VMEM_MIB = 24
SMEM = pl.BlockSpec(memory_space=pltpu.SMEM)
MOVES = (0, 1, 2, -1)


def pick(total, unit, most):
    size = total
    while size > most or total % size or size % unit:
        size -= unit
    return size


def whole(shape):
    return pl.BlockSpec(shape, lambda *i: (0,) * len(shape))


def shapes(*pairs):
    return [jax.ShapeDtypeStruct(shape, kind) for shape, kind in pairs]


def params(mib=VMEM_MIB):
    return pltpu.CompilerParams(vmem_limit_bytes=mib * 1024 * 1024)


def places(row_size, col_size):
    depth, width = row_size // 4, col_size // 2
    table = np.zeros((row_size * col_size, 16), np.int32)
    for index in range(row_size * col_size):
        row, col = divmod(index, col_size)
        slots = [(col // 2 + move) % width for move in MOVES] + [(row // 4 + move) % depth for move in MOVES]
        table[index, :12] = slots + [col % 2, row // 2 % 2, col, col // 2]
    return table


def assemble(own, chunk_refs, place_ref, base, parity, pair_ref, turned_ref, nodes_ref):
    extra = chunk_refs[0].shape[1] - own
    even = parity == 0
    blank = jnp.zeros((extra, 2 * own - chunk_refs[0].shape[2]), F32)
    for slot, chunk_ref in enumerate(chunk_refs):
        start = place_ref[base + slot] * 2 * own
        for flip in range(2):
            rows = pl.ds(pl.multiple_of(start + (parity ^ flip) * own, 64), own)
            pair_ref[rows, :] = chunk_ref[flip, :own, :]
        first = chunk_ref[0, own:, :].astype(F32)
        second = chunk_ref[1, own:, :].astype(F32)
        left = jnp.concatenate([jnp.where(even, first, second), blank], axis=1)
        right = jnp.concatenate([blank, jnp.where(even, second, first)], axis=1)
        both = left + pltpu.roll(right, own - blank.shape[1], 1)
        turned_ref[:extra, pl.ds(pl.multiple_of(start, LANES), 2 * own)] = both.astype(BF16)
    turned_ref[extra:, :] = jnp.zeros((LANES - extra, turned_ref.shape[1]), BF16)
    nodes_ref[...] = jnp.transpose(turned_ref[...])


def stats_kernel(own, feat, place_ref, *rest):
    parts = len(MOVES)
    a_refs, b0_refs, b1_refs = rest[0 : 2 * parts : 2], rest[1 : 2 * parts : 2], rest[2 * parts : 3 * parts]
    scaled_ref, stats_ref, a_pair, a_pair_t, a_src, a_src_t, b_pair, b_dst, b_dst_t, scores, peaks = rest[3 * parts :]
    step = pl.program_id(0)
    last = pl.num_programs(0) - 1
    count, cols = scores.shape
    span = pick(cols, LANES, 512)
    repeat = span // LANES

    def tiles(array):
        return [array[:, lane : lane + LANES] for lane in range(0, span, LANES)]

    def work(ahead, behind):
        block = step - 1 if behind else step
        here = pl.ds(pl.multiple_of(block * count, count), count)
        there = pl.ds(pl.multiple_of(step * count, count), count)
        total = jnp.zeros((count, LANES), F32)
        peak = jnp.zeros((count, LANES), F32)
        sums = jnp.zeros((count, 2 * feat), F32)
        for start in range(0, cols, span):
            part = slice(start, start + span)
            if behind:
                before = peaks[...]
                half = jnp.exp(scores[:, part] - jnp.concatenate([before] * repeat, axis=1)).astype(BF16)
                total = total + sum(tiles(half.astype(F32)))
                sums = sums + jnp.dot(half, b_pair[part, :], preferred_element_type=F32)
            if ahead:
                fresh = jnp.maximum(jnp.dot(a_src[there, :], b_dst_t[:, part], preferred_element_type=F32), 0.0)
                scores[:, part] = fresh
                peak = functools.reduce(jnp.maximum, tiles(fresh), peak)
        if behind:
            total = jnp.sum(total, axis=1, keepdims=True)
            sums = sums / total
            scaled_ref[...] = sums.astype(BF16)
            mates = a_pair[here, :].astype(F32)
            inner = jnp.sum(sums[:, :feat] * mates[:, feat:] + sums[:, feat:] * mates[:, :feat], axis=1, keepdims=True)
            lane = lax.broadcasted_iota(jnp.int32, (count, LANES), 1)
            table = jnp.where(lane == 0, peaks[...], jnp.where(lane == 1, total, inner))
            stats_ref[...] = jnp.broadcast_to(jnp.transpose(table)[:4][None], stats_ref.shape)
        if ahead:
            peaks[...] = jnp.broadcast_to(jnp.max(peak, axis=1, keepdims=True), peaks.shape)

    @pl.when(step == 0)
    def _():
        assemble(own, a_refs, place_ref, 0, place_ref[8], a_pair, a_src_t, a_src)
        half = b_pair.shape[0] // 2
        for index, b_refs in enumerate((b0_refs, b1_refs)):
            part = pl.ds(index * half, half)
            outs = (b_pair.at[part, :], b_dst_t.at[:, part], b_dst.at[part, :])
            assemble(own, b_refs, place_ref, 4, place_ref[9], *outs)
        a_pair_t[:feat] = jnp.transpose(a_pair[:, feat:])
        a_pair_t[feat:] = jnp.transpose(a_pair[:, :feat])
        work(True, False)

    @pl.when((step > 0) & (step < last))
    def _():
        work(True, True)

    @pl.when(step == last)
    def _():
        work(False, True)


def row_stats(place, a_parts, b0_parts, b1_parts, own, feat):
    mates = sum(part.shape[0] for part in a_parts)
    rows = mates * own
    cols = 2 * own * sum(part.shape[0] for part in b0_parts)
    pair = 2 * feat
    step = pick(rows, LANES, 512)
    kept = [((rows, pair), BF16), ((pair, rows), BF16), ((rows, LANES), BF16), ((LANES, rows), BF16)]
    kept += [((cols, pair), BF16), ((cols, LANES), BF16), ((LANES, cols), BF16)]
    parts = [part for both in zip(a_parts, b0_parts) for part in both] + b1_parts
    scaled, stats, *kept = pl.pallas_call(
        functools.partial(stats_kernel, own, feat),
        grid=(rows // step + 1,),
        in_specs=[SMEM] + [whole(x.shape) for x in parts],
        out_specs=[
            pl.BlockSpec((step, pair), lambda i: (jnp.maximum(i - 1, 0), 0)),
            pl.BlockSpec((mates, 4, step), lambda i: (0, 0, jnp.maximum(i - 1, 0))),
        ]
        + [whole(shape) for shape, kind in kept],
        out_shape=shapes(((rows, pair), BF16), ((mates, 4, rows), F32), *kept),
        scratch_shapes=[pltpu.VMEM((step, cols), F32), pltpu.VMEM((step, LANES), F32)],
        compiler_params=params(),
        cost_estimate=pl.CostEstimate(flops=2 * rows * cols * 512, bytes_accessed=8 << 20, transcendentals=rows * cols),
        name="row_stats",
    )(place, *parts)
    return scaled, stats, kept


def weigh_kernel(own, place_ref, stats_ref, scaled_ref, table_ref, mine_ref, given_ref, weights_ref):
    stats = stats_ref[...]
    peaks = stats[:, 0:1]
    peak = jnp.max(peaks, axis=0)
    weights = jnp.exp(peaks - peak[None]) * stats[:, 1:2]
    total = jnp.sum(weights, axis=0)
    table_ref[0:1, :] = peak + jnp.log(total)
    table_ref[1:2, :] = jnp.sum(weights * stats[:, 2:3], axis=0) / total
    table_ref[2:, :] = jnp.zeros((table_ref.shape[0] - 2, table_ref.shape[1]), F32)
    at = place_ref[10]
    weight = jnp.exp(stats_ref[at, 0:1] - peak) * stats_ref[at, 1:2] / total
    weights_ref[...] = jnp.transpose(jnp.broadcast_to(weight, (LANES, weight.shape[1])))
    for slot in range(mine_ref.shape[0]):
        for flip, out_ref in enumerate((mine_ref, given_ref)):
            chunk = 2 * (place_ref[11] ^ slot) + (place_ref[8] ^ flip)
            rows = pl.ds(pl.multiple_of(chunk * own, 64), own)
            out_ref[slot] = (weights_ref[rows, 0:1] * scaled_ref[rows, :].astype(F32)).astype(BF16)


def weigh(place, stats, scaled, own):
    rows, pair = scaled.shape
    count = stats.shape[0] // 2
    part = ((count, own, pair), BF16)
    return pl.pallas_call(
        functools.partial(weigh_kernel, own),
        in_specs=[SMEM] + [pl.BlockSpec(memory_space=pltpu.VMEM)] * 2,
        out_shape=shapes(((8, rows), F32), part, part),
        scratch_shapes=[pltpu.VMEM((rows, LANES), F32)],
        compiler_params=params(8),
        name="weigh",
    )(place, stats, scaled)


def tile_kernel(own, feat, half, place_ref, a_pair, a_pair_t, a_src, a_src_t, b_pair, b_dst, b_dst_t, table, *rest):
    pair = 2 * feat
    last = half == 0
    if last:
        start_ref, mine_ref, cols_ref, source_ref, *piece_refs, twin_ref = rest[:-5]
        col_sums, target_sums, scores, outer, slots = rest[-5:]
    else:
        cols_ref, source_ref, col_sums, target_sums, scores, outer = rest
    extra = cols_ref.shape[1] - own
    rows = a_pair.shape[0]
    cols = col_sums.shape[0]
    span = scores.shape[2]
    here = slice(half * cols, (half + 1) * cols)

    def ahead(index):
        part = slice(index * span, (index + 1) * span)
        scores[index % 2] = jnp.dot(b_dst[here, :], a_src_t[:, part], preferred_element_type=F32)
        outer[index % 2] = jnp.dot(b_pair[here, :], a_pair_t[:, part], preferred_element_type=F32)

    def behind(index):
        part = slice(index * span, (index + 1) * span)
        score = scores[index % 2]
        soft = jnp.exp(jnp.maximum(score, 0.0) - table[0:1, part])
        grad = jnp.where(score > 0.0, soft * (outer[index % 2] - table[1:2, part]), 0.0)
        soft_half = soft.astype(BF16)
        grad_half = grad.astype(BF16)
        more_cols = jnp.dot(soft_half, a_pair[part, :], preferred_element_type=F32)
        more_target = jnp.dot(grad_half, a_src[part, :], preferred_element_type=F32)
        more_source = jnp.dot(b_dst_t[:extra, here], grad_half, preferred_element_type=F32)
        col_sums[...] = col_sums[...] + more_cols if index else more_cols
        target_sums[...] = target_sums[...] + more_target if index else more_target
        source_ref[:, part] = start_ref[:, part] + more_source if last else more_source

    count = rows // span
    ahead(0)
    for index in range(count):
        if index + 1 < count:
            ahead(index + 1)
        behind(index)
    for slot in range(cols_ref.shape[0]):
        chunk = slice(slot * own, (slot + 1) * own)
        cols_ref[slot, :own, :] = col_sums[chunk, :].astype(BF16)
        wide = jnp.concatenate([target_sums[chunk, :], jnp.zeros((pair - own, LANES), F32)], axis=0)
        cols_ref[slot, own:, :] = jnp.transpose(wide)[:extra].astype(BF16)
    if last:
        fill = jnp.zeros((extra, pair - own), F32)
        for chunk in range(slots.shape[0]):
            part = source_ref[:, chunk * own : (chunk + 1) * own]
            slots[place_ref[10] ^ chunk] = jnp.concatenate([part, fill], axis=1)
        for slot, piece_ref in enumerate(piece_refs):
            piece_ref[:own, :] = mine_ref[slot]
            piece_ref[own:, :] = slots[2 * slot].astype(BF16)
            twin_ref[slot] = slots[2 * slot + 1].astype(BF16)


def tile_sums(place, kept, half, table, late, unread, own, feat, extra, name):
    rows, pair = kept[0].shape
    cols = kept[4].shape[0] // 2
    mates = rows // own
    span = pick(rows, LANES, 256)
    scratch = [pltpu.VMEM((cols, pair), F32), pltpu.VMEM((cols, LANES), F32)] + [pltpu.VMEM((2, cols, span), F32)] * 2
    kinds = []
    if half == 0:
        kinds = [((own + extra, pair), BF16)] * (mates // 2) + [((mates // 2, extra, pair), BF16)]
        scratch += [pltpu.VMEM((mates, extra, pair), F32)]
    vmem, anywhere = pl.BlockSpec(memory_space=pltpu.VMEM), pl.BlockSpec(memory_space=pl.ANY)
    work = 1 << 20 if half == 0 else 2 * rows * cols * 1280
    return pl.pallas_call(
        functools.partial(tile_kernel, own, feat, half),
        in_specs=[SMEM] + [vmem] * (len(kept) + 1 + len(late)) + [anywhere] * len(unread),
        out_shape=shapes(((cols // own, own + extra, pair), BF16), ((extra, rows), F32), *kinds),
        scratch_shapes=scratch,
        compiler_params=params(),
        cost_estimate=pl.CostEstimate(flops=work, bytes_accessed=1 << 20, transcendentals=work >> 11),
        name=name,
    )(place, *kept, table, *late, *unread)


def join_cols_kernel(own_ref, other_ref, unread_ref, out_ref):
    out_ref[...] = (own_ref[...].astype(F32) + other_ref[...].astype(F32)).astype(BF16)


def join_rows_kernel(given_ref, twin_ref, *rest):
    count, own = given_ref.shape[:2]
    for slot, (piece_ref, out_ref) in enumerate(zip(rest[:count], rest[count + 1 :])):
        out_ref[:own, :] = (piece_ref[:own, :].astype(F32) + given_ref[slot].astype(F32)).astype(BF16)
        out_ref[own:, :] = (piece_ref[own:, :].astype(F32) + twin_ref[slot].astype(F32)).astype(BF16)


def join(kernel, name, outs, *arrays, unread=()):
    vmem, anywhere = pl.BlockSpec(memory_space=pltpu.VMEM), pl.BlockSpec(memory_space=pl.ANY)
    return pl.pallas_call(
        kernel,
        in_specs=[vmem] * len(arrays) + [anywhere] * len(unread),
        out_shape=[jax.ShapeDtypeStruct(out.shape, out.dtype) for out in outs],
        compiler_params=params(8),
        name=name,
    )(*arrays, *unread)


def finish_kernel(own, feat, emb_count, cols_ref, *rest):
    piece_refs, (hop_ref, grad_ref, source_ref, target_ref) = rest[:-4], rest[-4:]
    total = jnp.zeros((own, 2 * feat), F32)
    extra = jnp.zeros((cols_ref.shape[1] - own, 2 * feat), F32)
    source = extra
    for piece_ref in piece_refs:
        total = total + piece_ref[:own, :].astype(F32)
        source = source + piece_ref[own:, :].astype(F32)
    for slot in range(cols_ref.shape[0]):
        total = total + cols_ref[slot, :own, :].astype(F32)
        extra = extra + cols_ref[slot, own:, :].astype(F32)
    hop_ref[...] = total[:, :feat].astype(BF16)
    grad_ref[...] = total[:, feat:].astype(BF16)
    source_ref[...] = source[:emb_count, :own]
    target_ref[...] = extra[:emb_count, :own]


def finish(cols, pieces, own, feat, emb_count):
    return pl.pallas_call(
        functools.partial(finish_kernel, own, feat, emb_count),
        out_shape=shapes(
            ((own, feat), BF16), ((own, feat), BF16), ((emb_count, own), F32), ((emb_count, own), F32)
        ),
        compiler_params=params(8),
        name="finish",
    )(cols, *pieces)


def local(sizes, source_embed, target_embed, features, cotangent):
    row_size, col_size = sizes
    emb_count, own = source_embed.shape
    feat = features.shape[1]
    pair = 2 * feat
    extra = -(-emb_count // 16) * 16
    depth, width = row_size // 4, col_size // 2
    both = ("row", "col")

    def device(z, y, core, x, skew):
        return (((z % depth) * 2 + y) * 2 + core) * col_size + (x % width) * 2 + (skew ^ y)

    groups = [
        [device(z, y, core, x, skew) for z in range(depth) for y in range(2)]
        for core in range(2) for x in range(width) for skew in range(2)
    ]

    def mate(array, bits):
        return lax.ppermute(array, "col", [(c, c ^ bits) for c in range(col_size)])

    def swap(array):
        return lax.ppermute(array, "row", [(r, r ^ 1) for r in range(row_size)])

    def along_x(array, move, flip):
        pairs = [(x * 2 + y, ((x + move) % width) * 2 + (y ^ flip)) for x in range(width) for y in range(2)]
        return lax.ppermute(array, "col", pairs)

    def along_z(array, move, flip):
        pairs = [
            (device(z, y, core, x, skew), device(z + move, y ^ flip, core, x, skew))
            for z in range(depth) for y in range(2) for core in range(2) for x in range(width) for skew in range(2)
        ]
        return lax.ppermute(array, both, pairs)

    def pack(embed):
        left = jnp.pad(features, ((0, extra), (0, feat)))
        right = jnp.pad(cotangent, ((0, extra), (feat, 0)))
        return left + right + jnp.pad(embed, ((own, extra - emb_count), (0, pair - own)))

    index = lax.axis_index(both)
    place = lax.dynamic_index_in_dim(jnp.asarray(places(row_size, col_size)), index, 0, keepdims=False)
    chunks, alongs = (pack(target_embed), pack(source_embed)), (along_z, along_x)
    near = [jnp.stack([chunk, along(chunk, 0, 1)]) for chunk, along in zip(chunks, alongs)]
    near, place = lax.optimization_barrier((near, place))
    right = [along(array, -1, 0) for array, along in zip(near, alongs)]
    far = [along(array, -1, 0) for array, along in zip(right, alongs)]
    left = [along(array, 1, 0) for array, along in zip(near, alongs)]
    b_parts, a_parts = [list(parts) for parts in zip(near, right, far, left)]
    others = [swap(part) for part in b_parts]
    scaled, stats, kept = row_stats(place, a_parts, b_parts, others, own, feat)
    stats = lax.all_to_all(stats, "col", 0, 0)

    sizes = (own, feat, extra)
    table, mine, *given = weigh(place, stats, scaled, own)
    given = [mate(part, 1) for part in given]
    other_cols, start = tile_sums(place, kept, 1, table, (), (), *sizes, "other_tile")
    other_cols = swap(other_cols)
    own_cols, unused, *pieces, twin = tile_sums(place, kept, 0, table, (start, mine), (), *sizes, "own_tile")
    twin = mate(twin, 1)
    (cols,) = join(join_cols_kernel, "join_cols", [own_cols], own_cols, other_cols, unread=given)
    pieces = join(join_rows_kernel, "join_rows", pieces, *given, twin, *pieces, unread=(cols,))
    cols = lax.all_to_all(cols, both, 0, 0, axis_index_groups=groups)
    pieces = [mate(piece, 2 * slot) if slot else piece for slot, piece in enumerate(pieces)]
    return tuple(finish(cols, pieces, own, feat, emb_count))


def solution(mesh):
    nodes = P(("row", "col"), None)
    embeds = P(None, ("row", "col"))
    sizes = (mesh.shape["row"], mesh.shape["col"])
    return jax.shard_map(
        functools.partial(local, sizes),
        mesh=mesh,
        in_specs=(embeds, embeds, nodes, nodes),
        out_specs=(nodes, nodes, embeds, embeds),
        check_vma=False,
    )
```

```python
import functools

import jax
import jax.numpy as jnp
import numpy as np
from jax import lax
from jax.experimental import pallas as pl
from jax.experimental.pallas import tpu as pltpu
from jax.sharding import PartitionSpec as P

F32 = jnp.float32
BF16 = jnp.bfloat16
LANES = 128
FULL, KEPT = 48, 32
VMEM_MIB = 24
SMEM = pl.BlockSpec(memory_space=pltpu.SMEM)
MOVES = (0, 1, 2, -1)


def pick(total, unit, most):
    size = total
    while size > most or total % size or size % unit:
        size -= unit
    return size


def whole(shape):
    return pl.BlockSpec(shape, lambda *i: (0,) * len(shape))


def shapes(*pairs):
    return [jax.ShapeDtypeStruct(shape, kind) for shape, kind in pairs]


def params(mib=VMEM_MIB):
    return pltpu.CompilerParams(vmem_limit_bytes=mib * 1024 * 1024)


def places(row_size, col_size):
    depth, width = row_size // 4, col_size // 2
    table = np.zeros((row_size * col_size, 16), np.int32)
    for index in range(row_size * col_size):
        row, col = divmod(index, col_size)
        slots = [(col // 2 + move) % width for move in MOVES] + [(row // 4 + move) % depth for move in MOVES]
        table[index, :12] = slots + [col % 2, row // 2 % 2, col, col // 2]
    return table


def fold(block):
    low, high = block[KEPT : KEPT + 8, :LANES], block[KEPT : KEPT + 8, LANES:]
    turned = [pltpu.roll(low, 64, 1), low, pltpu.roll(high, 64, 1), jnp.zeros_like(low)]
    lane = lax.broadcasted_iota(jnp.int32, (KEPT, LANES), 1)
    spare = jnp.where(lane >= 64, jnp.concatenate(turned, axis=0), block[:KEPT, LANES:])
    return jnp.concatenate([block[:KEPT, :LANES], spare], axis=1)


def unfold(block):
    lane = lax.broadcasted_iota(jnp.int32, (KEPT, LANES), 1)
    last = block[:, LANES:]
    spare = jnp.where(lane >= 64, last, 0.0)
    top = jnp.concatenate([block[:, :LANES], jnp.where(lane >= 64, 0.0, last)], axis=1)
    low = pltpu.roll(spare[0:8], 64, 1) + spare[8:16]
    bottom = jnp.concatenate([low, pltpu.roll(spare[16:24], 64, 1)], axis=1)
    return jnp.concatenate([top, bottom, jnp.zeros((FULL - KEPT - 8, block.shape[1]), F32)], axis=0)


def pack_kernel(source_hbm, target_hbm, feat_hbm, cot_hbm, a_ref, b_ref, source, target, feat, cot, wide, arrived):
    moves = ((source_hbm, source), (target_hbm, target), (feat_hbm, feat), (cot_hbm, cot))
    copies = [pltpu.make_async_copy(src, dst, arrived.at[index]) for index, (src, dst) in enumerate(moves)]
    for copy in copies:
        copy.start()
    for copy in copies:
        copy.wait()
    own, width = feat.shape
    for embed, out_ref in ((source, a_ref), (target, b_ref)):
        wide[...] = jnp.zeros(wide.shape, F32)
        wide[: embed.shape[0], :own] = embed[...].astype(F32)
        out_ref[:own, :width] = feat[...]
        out_ref[:own, width:] = cot[...]
        out_ref[own:, :] = fold(wide[...]).astype(BF16)


def pack(source_embed, target_embed, features, cotangent):
    own, feat = features.shape
    shape = (own + KEPT, 2 * feat)
    arrays = (source_embed, target_embed, features, cotangent)
    return pl.pallas_call(
        pack_kernel,
        in_specs=[pl.BlockSpec(memory_space=pltpu.HBM)] * len(arrays),
        out_shape=shapes((shape, BF16), (shape, BF16)),
        scratch_shapes=[pltpu.VMEM(array.shape, BF16) for array in arrays]
        + [pltpu.VMEM((FULL, 2 * feat), F32), pltpu.SemaphoreType.DMA((len(arrays),))],
        compiler_params=params(8),
        name="pack",
    )(*arrays)


def assemble(own, chunk_refs, place_ref, base, parity, pair_ref, turned_ref, nodes_ref):
    even = parity == 0
    blank = jnp.zeros((FULL, 2 * own - chunk_refs[0].shape[2]), F32)
    for slot, chunk_ref in enumerate(chunk_refs):
        start = place_ref[base + slot] * 2 * own
        for flip in range(2):
            rows = pl.ds(pl.multiple_of(start + (parity ^ flip) * own, 64), own)
            pair_ref[rows, :] = chunk_ref[flip, :own, :]
        first = unfold(chunk_ref[0, own:, :].astype(F32))
        second = unfold(chunk_ref[1, own:, :].astype(F32))
        left = jnp.concatenate([jnp.where(even, first, second), blank], axis=1)
        right = jnp.concatenate([blank, jnp.where(even, second, first)], axis=1)
        both = left + pltpu.roll(right, own - blank.shape[1], 1)
        turned_ref[:FULL, pl.ds(pl.multiple_of(start, LANES), 2 * own)] = both.astype(BF16)
    turned_ref[FULL:, :] = jnp.zeros((LANES - FULL, turned_ref.shape[1]), BF16)
    nodes_ref[...] = jnp.transpose(turned_ref[...])


def stats_kernel(own, feat, place_ref, *rest):
    parts = len(MOVES)
    a_refs, b0_refs, b1_refs = rest[0 : 2 * parts : 2], rest[1 : 2 * parts : 2], rest[2 * parts : 3 * parts]
    scaled_ref, stats_ref, a_pair, a_pair_t, a_src, a_src_t, b_pair, b_dst, b_dst_t, scores, peaks = rest[3 * parts :]
    step = pl.program_id(0)
    last = pl.num_programs(0) - 1
    count, cols = scores.shape
    span = pick(cols, LANES, 512)
    repeat = span // LANES

    def tiles(array):
        return [array[:, lane : lane + LANES] for lane in range(0, span, LANES)]

    def work(ahead, behind):
        block = step - 1 if behind else step
        here = pl.ds(pl.multiple_of(block * count, count), count)
        there = pl.ds(pl.multiple_of(step * count, count), count)
        total = jnp.zeros((count, LANES), F32)
        peak = jnp.zeros((count, LANES), F32)
        sums = jnp.zeros((count, 2 * feat), F32)
        for start in range(0, cols, span):
            part = slice(start, start + span)
            if behind:
                before = peaks[...]
                half = jnp.exp(scores[:, part] - jnp.concatenate([before] * repeat, axis=1)).astype(BF16)
                total = total + sum(tiles(half.astype(F32)))
                sums = sums + jnp.dot(half, b_pair[part, :], preferred_element_type=F32)
            if ahead:
                fresh = jnp.maximum(jnp.dot(a_src[there, :], b_dst_t[:, part], preferred_element_type=F32), 0.0)
                scores[:, part] = fresh
                peak = functools.reduce(jnp.maximum, tiles(fresh), peak)
        if behind:
            total = jnp.sum(total, axis=1, keepdims=True)
            sums = sums / total
            scaled_ref[...] = sums.astype(BF16)
            mates = a_pair[here, :].astype(F32)
            inner = jnp.sum(sums[:, :feat] * mates[:, feat:] + sums[:, feat:] * mates[:, :feat], axis=1, keepdims=True)
            lane = lax.broadcasted_iota(jnp.int32, (count, LANES), 1)
            table = jnp.where(lane == 0, peaks[...], jnp.where(lane == 1, total, inner))
            stats_ref[...] = jnp.broadcast_to(jnp.transpose(table)[:4][None], stats_ref.shape)
        if ahead:
            peaks[...] = jnp.broadcast_to(jnp.max(peak, axis=1, keepdims=True), peaks.shape)

    @pl.when(step == 0)
    def _():
        assemble(own, a_refs, place_ref, 0, place_ref[8], a_pair, a_src_t, a_src)
        half = b_pair.shape[0] // 2
        for index, b_refs in enumerate((b0_refs, b1_refs)):
            part = pl.ds(index * half, half)
            outs = (b_pair.at[part, :], b_dst_t.at[:, part], b_dst.at[part, :])
            assemble(own, b_refs, place_ref, 4, place_ref[9], *outs)
        a_pair_t[:feat] = jnp.transpose(a_pair[:, feat:])
        a_pair_t[feat:] = jnp.transpose(a_pair[:, :feat])
        work(True, False)

    @pl.when((step > 0) & (step < last))
    def _():
        work(True, True)

    @pl.when(step == last)
    def _():
        work(False, True)


def row_stats(place, a_parts, b0_parts, b1_parts, own, feat):
    mates = sum(part.shape[0] for part in a_parts)
    rows = mates * own
    cols = 2 * own * sum(part.shape[0] for part in b0_parts)
    pair = 2 * feat
    step = pick(rows, LANES, 512)
    kept = [((rows, pair), BF16), ((pair, rows), BF16), ((rows, LANES), BF16), ((LANES, rows), BF16)]
    kept += [((cols, pair), BF16), ((cols, LANES), BF16), ((LANES, cols), BF16)]
    parts = [part for both in zip(a_parts, b0_parts) for part in both] + b1_parts
    scaled, stats, *kept = pl.pallas_call(
        functools.partial(stats_kernel, own, feat),
        grid=(rows // step + 1,),
        in_specs=[SMEM] + [whole(x.shape) for x in parts],
        out_specs=[
            pl.BlockSpec((step, pair), lambda i: (jnp.maximum(i - 1, 0), 0)),
            pl.BlockSpec((mates, 4, step), lambda i: (0, 0, jnp.maximum(i - 1, 0))),
        ]
        + [whole(shape) for shape, kind in kept],
        out_shape=shapes(((rows, pair), BF16), ((mates, 4, rows), F32), *kept),
        scratch_shapes=[pltpu.VMEM((step, cols), F32), pltpu.VMEM((step, LANES), F32)],
        compiler_params=params(),
        cost_estimate=pl.CostEstimate(flops=2 * rows * cols * 512, bytes_accessed=8 << 20, transcendentals=rows * cols),
        name="row_stats",
    )(place, *parts)
    return scaled, stats, kept


def weigh_kernel(own, place_ref, stats_ref, scaled_ref, table_ref, mine_ref, given_ref, weights_ref):
    stats = stats_ref[...]
    peaks = stats[:, 0:1]
    peak = jnp.max(peaks, axis=0)
    weights = jnp.exp(peaks - peak[None]) * stats[:, 1:2]
    total = jnp.sum(weights, axis=0)
    table_ref[0:1, :] = peak + jnp.log(total)
    table_ref[1:2, :] = jnp.sum(weights * stats[:, 2:3], axis=0) / total
    table_ref[2:, :] = jnp.zeros((table_ref.shape[0] - 2, table_ref.shape[1]), F32)
    at = place_ref[10]
    weight = jnp.exp(stats_ref[at, 0:1] - peak) * stats_ref[at, 1:2] / total
    weights_ref[...] = jnp.transpose(jnp.broadcast_to(weight, (LANES, weight.shape[1])))
    for slot in range(mine_ref.shape[0]):
        for flip, out_ref in enumerate((mine_ref, given_ref)):
            chunk = 2 * (place_ref[11] ^ slot) + (place_ref[8] ^ flip)
            rows = pl.ds(pl.multiple_of(chunk * own, 64), own)
            out_ref[slot] = (weights_ref[rows, 0:1] * scaled_ref[rows, :].astype(F32)).astype(BF16)


def weigh(place, stats, scaled, own):
    rows, pair = scaled.shape
    count = stats.shape[0] // 2
    part = ((count, own, pair), BF16)
    return pl.pallas_call(
        functools.partial(weigh_kernel, own),
        in_specs=[SMEM] + [pl.BlockSpec(memory_space=pltpu.VMEM)] * 2,
        out_shape=shapes(((8, rows), F32), part, part),
        scratch_shapes=[pltpu.VMEM((rows, LANES), F32)],
        compiler_params=params(8),
        name="weigh",
    )(place, stats, scaled)


def tile_kernel(own, feat, half, place_ref, a_pair, a_pair_t, a_src, a_src_t, b_pair, b_dst, b_dst_t, table, *rest):
    pair = 2 * feat
    last = half == 0
    if last:
        start_ref, mine_ref, cols_ref, source_ref, *piece_refs, twin_ref = rest[:-5]
        col_sums, target_sums, scores, outer, slots = rest[-5:]
    else:
        cols_ref, source_ref, col_sums, target_sums, scores, outer = rest
    rows = a_pair.shape[0]
    cols = col_sums.shape[0]
    span = scores.shape[2]
    here = slice(half * cols, (half + 1) * cols)

    def ahead(index):
        part = slice(index * span, (index + 1) * span)
        scores[index % 2] = jnp.dot(b_dst[here, :], a_src_t[:, part], preferred_element_type=F32)
        outer[index % 2] = jnp.dot(b_pair[here, :], a_pair_t[:, part], preferred_element_type=F32)

    def behind(index):
        part = slice(index * span, (index + 1) * span)
        score = scores[index % 2]
        soft = jnp.exp(jnp.maximum(score, 0.0) - table[0:1, part])
        grad = jnp.where(score > 0.0, soft * (outer[index % 2] - table[1:2, part]), 0.0)
        soft_half = soft.astype(BF16)
        grad_half = grad.astype(BF16)
        more_cols = jnp.dot(soft_half, a_pair[part, :], preferred_element_type=F32)
        more_target = jnp.dot(grad_half, a_src[part, :], preferred_element_type=F32)
        more_source = jnp.dot(b_dst_t[:FULL, here], grad_half, preferred_element_type=F32)
        col_sums[...] = col_sums[...] + more_cols if index else more_cols
        target_sums[...] = target_sums[...] + more_target if index else more_target
        source_ref[:, part] = start_ref[:, part] + more_source if last else more_source

    count = rows // span
    ahead(0)
    for index in range(count):
        if index + 1 < count:
            ahead(index + 1)
        behind(index)
    for slot in range(cols_ref.shape[0]):
        chunk = slice(slot * own, (slot + 1) * own)
        cols_ref[slot, :own, :] = col_sums[chunk, :].astype(BF16)
        wide = jnp.concatenate([target_sums[chunk, :], jnp.zeros((pair - own, LANES), F32)], axis=0)
        cols_ref[slot, own:, :] = fold(jnp.transpose(wide)[:FULL]).astype(BF16)
    if last:
        fill = jnp.zeros((FULL, pair - own), F32)
        for chunk in range(slots.shape[0]):
            part = source_ref[:, chunk * own : (chunk + 1) * own]
            slots[place_ref[10] ^ chunk] = fold(jnp.concatenate([part, fill], axis=1))
        for slot, piece_ref in enumerate(piece_refs):
            piece_ref[:own, :] = mine_ref[slot]
            piece_ref[own:, :] = slots[2 * slot].astype(BF16)
            twin_ref[slot] = slots[2 * slot + 1].astype(BF16)


def tile_sums(place, kept, half, table, late, unread, own, feat, name):
    rows, pair = kept[0].shape
    cols = kept[4].shape[0] // 2
    mates = rows // own
    span = pick(rows, LANES, 256)
    scratch = [pltpu.VMEM((cols, pair), F32), pltpu.VMEM((cols, LANES), F32)] + [pltpu.VMEM((2, cols, span), F32)] * 2
    kinds = []
    if half == 0:
        kinds = [((own + KEPT, pair), BF16)] * (mates // 2) + [((mates // 2, KEPT, pair), BF16)]
        scratch += [pltpu.VMEM((mates, KEPT, pair), F32)]
    vmem, anywhere = pl.BlockSpec(memory_space=pltpu.VMEM), pl.BlockSpec(memory_space=pl.ANY)
    work = 1 << 20 if half == 0 else 2 * rows * cols * 1280
    return pl.pallas_call(
        functools.partial(tile_kernel, own, feat, half),
        in_specs=[SMEM] + [vmem] * (len(kept) + 1 + len(late)) + [anywhere] * len(unread),
        out_shape=shapes(((cols // own, own + KEPT, pair), BF16), ((FULL, rows), F32), *kinds),
        scratch_shapes=scratch,
        compiler_params=params(),
        cost_estimate=pl.CostEstimate(flops=work, bytes_accessed=1 << 20, transcendentals=work >> 11),
        name=name,
    )(place, *kept, table, *late, *unread)


def join_cols_kernel(own_ref, other_ref, unread_ref, out_ref):
    out_ref[...] = (own_ref[...].astype(F32) + other_ref[...].astype(F32)).astype(BF16)


def join_rows_kernel(given_ref, twin_ref, *rest):
    count, own = given_ref.shape[:2]
    for slot, (piece_ref, out_ref) in enumerate(zip(rest[:count], rest[count + 1 :])):
        out_ref[:own, :] = (piece_ref[:own, :].astype(F32) + given_ref[slot].astype(F32)).astype(BF16)
        out_ref[own:, :] = (piece_ref[own:, :].astype(F32) + twin_ref[slot].astype(F32)).astype(BF16)


def join(kernel, name, outs, *arrays, unread=()):
    vmem, anywhere = pl.BlockSpec(memory_space=pltpu.VMEM), pl.BlockSpec(memory_space=pl.ANY)
    return pl.pallas_call(
        kernel,
        in_specs=[vmem] * len(arrays) + [anywhere] * len(unread),
        out_shape=[jax.ShapeDtypeStruct(out.shape, out.dtype) for out in outs],
        compiler_params=params(8),
        name=name,
    )(*arrays, *unread)


def finish_kernel(own, feat, emb_count, cols_ref, *rest):
    piece_refs, (hop_ref, grad_ref, source_ref, target_ref) = rest[:-4], rest[-4:]
    total = jnp.zeros((own, 2 * feat), F32)
    extra = jnp.zeros((cols_ref.shape[1] - own, 2 * feat), F32)
    source = extra
    for piece_ref in piece_refs:
        total = total + piece_ref[:own, :].astype(F32)
        source = source + piece_ref[own:, :].astype(F32)
    for slot in range(cols_ref.shape[0]):
        total = total + cols_ref[slot, :own, :].astype(F32)
        extra = extra + cols_ref[slot, own:, :].astype(F32)
    hop_ref[...] = total[:, :feat].astype(BF16)
    grad_ref[...] = total[:, feat:].astype(BF16)
    source_ref[...] = unfold(source)[:emb_count, :own]
    target_ref[...] = unfold(extra)[:emb_count, :own]


def finish(cols, pieces, own, feat, emb_count):
    return pl.pallas_call(
        functools.partial(finish_kernel, own, feat, emb_count),
        out_shape=shapes(
            ((own, feat), BF16), ((own, feat), BF16), ((emb_count, own), F32), ((emb_count, own), F32)
        ),
        compiler_params=params(8),
        name="finish",
    )(cols, *pieces)


def local(sizes, source_embed, target_embed, features, cotangent):
    row_size, col_size = sizes
    emb_count, own = source_embed.shape
    feat = features.shape[1]
    pair = 2 * feat
    depth, width = row_size // 4, col_size // 2
    both = ("row", "col")

    def device(z, y, core, x, skew):
        return (((z % depth) * 2 + y) * 2 + core) * col_size + (x % width) * 2 + (skew ^ y)

    groups = [
        [device(z, y, core, x, skew) for z in range(depth) for y in range(2)]
        for core in range(2) for x in range(width) for skew in range(2)
    ]

    def mate(array, bits):
        return lax.ppermute(array, "col", [(c, c ^ bits) for c in range(col_size)])

    def swap(array):
        return lax.ppermute(array, "row", [(r, r ^ 1) for r in range(row_size)])

    def along_x(array, move, flip):
        pairs = [(x * 2 + y, ((x + move) % width) * 2 + (y ^ flip)) for x in range(width) for y in range(2)]
        return lax.ppermute(array, "col", pairs)

    def along_z(array, move, flip):
        pairs = [
            (device(z, y, core, x, skew), device(z + move, y ^ flip, core, x, skew))
            for z in range(depth) for y in range(2) for core in range(2) for x in range(width) for skew in range(2)
        ]
        return lax.ppermute(array, both, pairs)

    index = lax.axis_index(both)
    place = lax.dynamic_index_in_dim(jnp.asarray(places(row_size, col_size)), index, 0, keepdims=False)
    pack_a, pack_b = pack(source_embed, target_embed, features, cotangent)
    chunks, alongs = (pack_b, pack_a), (along_z, along_x)
    near = [jnp.stack([chunk, along(chunk, 0, 1)]) for chunk, along in zip(chunks, alongs)]
    near, place = lax.optimization_barrier((near, place))
    moved = [[along(array, -move, 0) for array, along in zip(near, alongs)] for move in MOVES[1:]]
    b_parts, a_parts = [[array, *[pair[index] for pair in moved]] for index, array in enumerate(near)]
    others = [swap(part) for part in b_parts]
    scaled, stats, kept = row_stats(place, a_parts, b_parts, others, own, feat)
    stats = lax.all_to_all(stats, "col", 0, 0)

    sizes = (own, feat)
    table, mine, *given = weigh(place, stats, scaled, own)
    given = [mate(part, 1) for part in given]
    other_cols, start = tile_sums(place, kept, 1, table, (), (), *sizes, "other_tile")
    other_cols = swap(other_cols)
    own_cols, unused, *pieces, twin = tile_sums(place, kept, 0, table, (start, mine), (), *sizes, "own_tile")
    twin = mate(twin, 1)
    (cols,) = join(join_cols_kernel, "join_cols", [own_cols], own_cols, other_cols, unread=given)
    pieces = join(join_rows_kernel, "join_rows", pieces, *given, twin, *pieces, unread=(cols,))
    cols = lax.all_to_all(cols, both, 0, 0, axis_index_groups=groups)
    pieces = [mate(piece, 2 * slot) if slot else piece for slot, piece in enumerate(pieces)]
    return tuple(finish(cols, pieces, own, feat, emb_count))


def solution(mesh):
    nodes = P(("row", "col"), None)
    embeds = P(None, ("row", "col"))
    sizes = (mesh.shape["row"], mesh.shape["col"])
    return jax.shard_map(
        functools.partial(local, sizes),
        mesh=mesh,
        in_specs=(embeds, embeds, nodes, nodes),
        out_specs=(nodes, nodes, embeds, embeds),
        check_vma=False,
    )
```

```python
import functools

import jax
import jax.numpy as jnp
import numpy as np
from jax import lax
from jax.experimental import pallas as pl
from jax.experimental.pallas import tpu as pltpu
from jax.sharding import PartitionSpec as P

F32 = jnp.float32
BF16 = jnp.bfloat16
LANES = 128
FULL, KEPT = 48, 32
VMEM_MIB = 24
SMEM = pl.BlockSpec(memory_space=pltpu.SMEM)
MOVES = (0, 1, 2, -1)


def pick(total, unit, most):
    size = total
    while size > most or total % size or size % unit:
        size -= unit
    return size


def whole(shape):
    return pl.BlockSpec(shape, lambda *i: (0,) * len(shape))


def shapes(*pairs):
    return [jax.ShapeDtypeStruct(shape, kind) for shape, kind in pairs]


def params(mib=VMEM_MIB):
    return pltpu.CompilerParams(vmem_limit_bytes=mib * 1024 * 1024)


def places(row_size, col_size):
    depth, width = row_size // 4, col_size // 2
    table = np.zeros((row_size * col_size, 16), np.int32)
    for index in range(row_size * col_size):
        row, col = divmod(index, col_size)
        slots = [(col // 2 + move) % width for move in MOVES] + [(row // 4 + move) % depth for move in MOVES]
        table[index, :12] = slots + [col % 2, row // 2 % 2, col, col // 2]
    return table


def fold(block):
    low, high = block[KEPT : KEPT + 8, :LANES], block[KEPT : KEPT + 8, LANES:]
    turned = [pltpu.roll(low, 64, 1), low, pltpu.roll(high, 64, 1), jnp.zeros_like(low)]
    lane = lax.broadcasted_iota(jnp.int32, (KEPT, LANES), 1)
    spare = jnp.where(lane >= 64, jnp.concatenate(turned, axis=0), block[:KEPT, LANES:])
    return jnp.concatenate([block[:KEPT, :LANES], spare], axis=1)


def unfold(block):
    lane = lax.broadcasted_iota(jnp.int32, (KEPT, LANES), 1)
    last = block[:, LANES:]
    spare = jnp.where(lane >= 64, last, 0.0)
    top = jnp.concatenate([block[:, :LANES], jnp.where(lane >= 64, 0.0, last)], axis=1)
    low = pltpu.roll(spare[0:8], 64, 1) + spare[8:16]
    bottom = jnp.concatenate([low, pltpu.roll(spare[16:24], 64, 1)], axis=1)
    return jnp.concatenate([top, bottom, jnp.zeros((FULL - KEPT - 8, block.shape[1]), F32)], axis=0)


def assemble(own, chunk_refs, place_ref, base, parity, pair_ref, turned_ref, nodes_ref):
    even = parity == 0
    blank = jnp.zeros((FULL, 2 * own - chunk_refs[0].shape[2]), F32)
    for slot, chunk_ref in enumerate(chunk_refs):
        start = place_ref[base + slot] * 2 * own
        for flip in range(2):
            rows = pl.ds(pl.multiple_of(start + (parity ^ flip) * own, 64), own)
            pair_ref[rows, :] = chunk_ref[flip, :own, :]
        first = unfold(chunk_ref[0, own:, :].astype(F32))
        second = unfold(chunk_ref[1, own:, :].astype(F32))
        left = jnp.concatenate([jnp.where(even, first, second), blank], axis=1)
        right = jnp.concatenate([blank, jnp.where(even, second, first)], axis=1)
        both = left + pltpu.roll(right, own - blank.shape[1], 1)
        turned_ref[:FULL, pl.ds(pl.multiple_of(start, LANES), 2 * own)] = both.astype(BF16)
    turned_ref[FULL:, :] = jnp.zeros((LANES - FULL, turned_ref.shape[1]), BF16)
    nodes_ref[...] = jnp.transpose(turned_ref[...])


def stats_kernel(own, feat, place_ref, *rest):
    parts = len(MOVES)
    a_refs, b0_refs, b1_refs = rest[0 : 2 * parts : 2], rest[1 : 2 * parts : 2], rest[2 * parts : 3 * parts]
    scaled_ref, stats_ref, a_pair, a_pair_t, a_src, a_src_t, b_pair, b_dst, b_dst_t, scores, peaks = rest[3 * parts :]
    step = pl.program_id(0)
    last = pl.num_programs(0) - 1
    count, cols = scores.shape
    span = pick(cols, LANES, 512)
    repeat = span // LANES

    def tiles(array):
        return [array[:, lane : lane + LANES] for lane in range(0, span, LANES)]

    def work(ahead, behind):
        block = step - 1 if behind else step
        here = pl.ds(pl.multiple_of(block * count, count), count)
        there = pl.ds(pl.multiple_of(step * count, count), count)
        total = jnp.zeros((count, LANES), F32)
        peak = jnp.zeros((count, LANES), F32)
        sums = jnp.zeros((count, 2 * feat), F32)
        for start in range(0, cols, span):
            part = slice(start, start + span)
            if behind:
                before = peaks[...]
                half = jnp.exp(scores[:, part] - jnp.concatenate([before] * repeat, axis=1)).astype(BF16)
                total = total + sum(tiles(half.astype(F32)))
                sums = sums + jnp.dot(half, b_pair[part, :], preferred_element_type=F32)
            if ahead:
                fresh = jnp.maximum(jnp.dot(a_src[there, :], b_dst_t[:, part], preferred_element_type=F32), 0.0)
                scores[:, part] = fresh
                peak = functools.reduce(jnp.maximum, tiles(fresh), peak)
        if behind:
            total = jnp.sum(total, axis=1, keepdims=True)
            sums = sums / total
            scaled_ref[...] = sums.astype(BF16)
            mates = a_pair[here, :].astype(F32)
            inner = jnp.sum(sums[:, :feat] * mates[:, feat:] + sums[:, feat:] * mates[:, :feat], axis=1, keepdims=True)
            lane = lax.broadcasted_iota(jnp.int32, (count, LANES), 1)
            table = jnp.where(lane == 0, peaks[...], jnp.where(lane == 1, total, inner))
            stats_ref[...] = jnp.broadcast_to(jnp.transpose(table)[:4][None], stats_ref.shape)
        if ahead:
            peaks[...] = jnp.broadcast_to(jnp.max(peak, axis=1, keepdims=True), peaks.shape)

    @pl.when(step == 0)
    def _():
        assemble(own, a_refs, place_ref, 0, place_ref[8], a_pair, a_src_t, a_src)
        half = b_pair.shape[0] // 2
        for index, b_refs in enumerate((b0_refs, b1_refs)):
            part = pl.ds(index * half, half)
            outs = (b_pair.at[part, :], b_dst_t.at[:, part], b_dst.at[part, :])
            assemble(own, b_refs, place_ref, 4, place_ref[9], *outs)
        a_pair_t[:feat] = jnp.transpose(a_pair[:, feat:])
        a_pair_t[feat:] = jnp.transpose(a_pair[:, :feat])
        work(True, False)

    @pl.when((step > 0) & (step < last))
    def _():
        work(True, True)

    @pl.when(step == last)
    def _():
        work(False, True)


def row_stats(place, a_parts, b0_parts, b1_parts, own, feat):
    mates = sum(part.shape[0] for part in a_parts)
    rows = mates * own
    cols = 2 * own * sum(part.shape[0] for part in b0_parts)
    pair = 2 * feat
    step = pick(rows, LANES, 512)
    kept = [((rows, pair), BF16), ((pair, rows), BF16), ((rows, LANES), BF16), ((LANES, rows), BF16)]
    kept += [((cols, pair), BF16), ((cols, LANES), BF16), ((LANES, cols), BF16)]
    parts = [part for both in zip(a_parts, b0_parts) for part in both] + b1_parts
    scaled, stats, *kept = pl.pallas_call(
        functools.partial(stats_kernel, own, feat),
        grid=(rows // step + 1,),
        in_specs=[SMEM] + [whole(x.shape) for x in parts],
        out_specs=[
            pl.BlockSpec((step, pair), lambda i: (jnp.maximum(i - 1, 0), 0)),
            pl.BlockSpec((mates, 4, step), lambda i: (0, 0, jnp.maximum(i - 1, 0))),
        ]
        + [whole(shape) for shape, kind in kept],
        out_shape=shapes(((rows, pair), BF16), ((mates, 4, rows), F32), *kept),
        scratch_shapes=[pltpu.VMEM((step, cols), F32), pltpu.VMEM((step, LANES), F32)],
        compiler_params=params(),
        cost_estimate=pl.CostEstimate(flops=2 * rows * cols * 512, bytes_accessed=8 << 20, transcendentals=rows * cols),
        name="row_stats",
    )(place, *parts)
    return scaled, stats, kept


def weigh_kernel(own, place_ref, stats_ref, scaled_ref, table_ref, mine_ref, given_ref, weights_ref):
    stats = stats_ref[...]
    peaks = stats[:, 0:1]
    peak = jnp.max(peaks, axis=0)
    weights = jnp.exp(peaks - peak[None]) * stats[:, 1:2]
    total = jnp.sum(weights, axis=0)
    table_ref[0:1, :] = peak + jnp.log(total)
    table_ref[1:2, :] = jnp.sum(weights * stats[:, 2:3], axis=0) / total
    table_ref[2:, :] = jnp.zeros((table_ref.shape[0] - 2, table_ref.shape[1]), F32)
    at = place_ref[10]
    weight = jnp.exp(stats_ref[at, 0:1] - peak) * stats_ref[at, 1:2] / total
    weights_ref[...] = jnp.transpose(jnp.broadcast_to(weight, (LANES, weight.shape[1])))
    for slot in range(mine_ref.shape[0]):
        for flip, out_ref in enumerate((mine_ref, given_ref)):
            chunk = 2 * (place_ref[11] ^ slot) + (place_ref[8] ^ flip)
            rows = pl.ds(pl.multiple_of(chunk * own, 64), own)
            out_ref[slot] = (weights_ref[rows, 0:1] * scaled_ref[rows, :].astype(F32)).astype(BF16)


def weigh(place, stats, scaled, own):
    rows, pair = scaled.shape
    count = stats.shape[0] // 2
    part = ((count, own, pair), BF16)
    return pl.pallas_call(
        functools.partial(weigh_kernel, own),
        in_specs=[SMEM] + [pl.BlockSpec(memory_space=pltpu.VMEM)] * 2,
        out_shape=shapes(((8, rows), F32), part, part),
        scratch_shapes=[pltpu.VMEM((rows, LANES), F32)],
        compiler_params=params(8),
        name="weigh",
    )(place, stats, scaled)


def tile_kernel(own, feat, half, place_ref, a_pair, a_pair_t, a_src, a_src_t, b_pair, b_dst, b_dst_t, table, *rest):
    pair = 2 * feat
    last = half == 0
    if last:
        start_ref, mine_ref, cols_ref, source_ref, *piece_refs, twin_ref = rest[:-5]
        col_sums, target_sums, scores, outer, slots = rest[-5:]
    else:
        cols_ref, source_ref, col_sums, target_sums, scores, outer = rest
    rows = a_pair.shape[0]
    cols = col_sums.shape[0]
    span = scores.shape[2]
    here = slice(half * cols, (half + 1) * cols)

    def ahead(index):
        part = slice(index * span, (index + 1) * span)
        scores[index % 2] = jnp.dot(b_dst[here, :], a_src_t[:, part], preferred_element_type=F32)
        outer[index % 2] = jnp.dot(b_pair[here, :], a_pair_t[:, part], preferred_element_type=F32)

    def behind(index):
        part = slice(index * span, (index + 1) * span)
        score = scores[index % 2]
        soft = jnp.exp(jnp.maximum(score, 0.0) - table[0:1, part])
        grad = jnp.where(score > 0.0, soft * (outer[index % 2] - table[1:2, part]), 0.0)
        soft_half = soft.astype(BF16)
        grad_half = grad.astype(BF16)
        more_cols = jnp.dot(soft_half, a_pair[part, :], preferred_element_type=F32)
        more_target = jnp.dot(grad_half, a_src[part, :], preferred_element_type=F32)
        more_source = jnp.dot(b_dst_t[:FULL, here], grad_half, preferred_element_type=F32)
        col_sums[...] = col_sums[...] + more_cols if index else more_cols
        target_sums[...] = target_sums[...] + more_target if index else more_target
        source_ref[:, part] = start_ref[:, part] + more_source if last else more_source

    count = rows // span
    ahead(0)
    for index in range(count):
        if index + 1 < count:
            ahead(index + 1)
        behind(index)
    for slot in range(cols_ref.shape[0]):
        chunk = slice(slot * own, (slot + 1) * own)
        cols_ref[slot, :own, :] = col_sums[chunk, :].astype(BF16)
        wide = jnp.concatenate([target_sums[chunk, :], jnp.zeros((pair - own, LANES), F32)], axis=0)
        cols_ref[slot, own:, :] = fold(jnp.transpose(wide)[:FULL]).astype(BF16)
    if last:
        fill = jnp.zeros((FULL, pair - own), F32)
        for chunk in range(slots.shape[0]):
            part = source_ref[:, chunk * own : (chunk + 1) * own]
            slots[place_ref[10] ^ chunk] = fold(jnp.concatenate([part, fill], axis=1))
        for slot, piece_ref in enumerate(piece_refs):
            piece_ref[:own, :] = mine_ref[slot]
            piece_ref[own:, :] = slots[2 * slot].astype(BF16)
            twin_ref[slot] = slots[2 * slot + 1].astype(BF16)


def tile_sums(place, kept, half, table, late, unread, own, feat, name):
    rows, pair = kept[0].shape
    cols = kept[4].shape[0] // 2
    mates = rows // own
    span = pick(rows, LANES, 256)
    scratch = [pltpu.VMEM((cols, pair), F32), pltpu.VMEM((cols, LANES), F32)] + [pltpu.VMEM((2, cols, span), F32)] * 2
    kinds = []
    if half == 0:
        kinds = [((own + KEPT, pair), BF16)] * (mates // 2) + [((mates // 2, KEPT, pair), BF16)]
        scratch += [pltpu.VMEM((mates, KEPT, pair), F32)]
    vmem, anywhere = pl.BlockSpec(memory_space=pltpu.VMEM), pl.BlockSpec(memory_space=pl.ANY)
    work = 1 << 20 if half == 0 else 2 * rows * cols * 1280
    return pl.pallas_call(
        functools.partial(tile_kernel, own, feat, half),
        in_specs=[SMEM] + [vmem] * (len(kept) + 1 + len(late)) + [anywhere] * len(unread),
        out_shape=shapes(((cols // own, own + KEPT, pair), BF16), ((FULL, rows), F32), *kinds),
        scratch_shapes=scratch,
        compiler_params=params(),
        cost_estimate=pl.CostEstimate(flops=work, bytes_accessed=1 << 20, transcendentals=work >> 11),
        name=name,
    )(place, *kept, table, *late, *unread)


def join_cols_kernel(own_ref, other_ref, unread_ref, out_ref):
    out_ref[...] = (own_ref[...].astype(F32) + other_ref[...].astype(F32)).astype(BF16)


def join_rows_kernel(given_ref, twin_ref, *rest):
    count, own = given_ref.shape[:2]
    for slot, (piece_ref, out_ref) in enumerate(zip(rest[:count], rest[count + 1 :])):
        out_ref[:own, :] = (piece_ref[:own, :].astype(F32) + given_ref[slot].astype(F32)).astype(BF16)
        out_ref[own:, :] = (piece_ref[own:, :].astype(F32) + twin_ref[slot].astype(F32)).astype(BF16)


def join(kernel, name, outs, *arrays, unread=()):
    vmem, anywhere = pl.BlockSpec(memory_space=pltpu.VMEM), pl.BlockSpec(memory_space=pl.ANY)
    return pl.pallas_call(
        kernel,
        in_specs=[vmem] * len(arrays) + [anywhere] * len(unread),
        out_shape=[jax.ShapeDtypeStruct(out.shape, out.dtype) for out in outs],
        compiler_params=params(8),
        name=name,
    )(*arrays, *unread)


def finish_kernel(own, feat, emb_count, cols_ref, *rest):
    piece_refs, (hop_ref, grad_ref, source_ref, target_ref) = rest[:-4], rest[-4:]
    total = jnp.zeros((own, 2 * feat), F32)
    extra = jnp.zeros((cols_ref.shape[1] - own, 2 * feat), F32)
    source = extra
    for piece_ref in piece_refs:
        total = total + piece_ref[:own, :].astype(F32)
        source = source + piece_ref[own:, :].astype(F32)
    for slot in range(cols_ref.shape[0]):
        total = total + cols_ref[slot, :own, :].astype(F32)
        extra = extra + cols_ref[slot, own:, :].astype(F32)
    hop_ref[...] = total[:, :feat].astype(BF16)
    grad_ref[...] = total[:, feat:].astype(BF16)
    source_ref[...] = unfold(source)[:emb_count, :own]
    target_ref[...] = unfold(extra)[:emb_count, :own]


def finish(cols, pieces, own, feat, emb_count):
    return pl.pallas_call(
        functools.partial(finish_kernel, own, feat, emb_count),
        out_shape=shapes(
            ((own, feat), BF16), ((own, feat), BF16), ((emb_count, own), F32), ((emb_count, own), F32)
        ),
        compiler_params=params(8),
        name="finish",
    )(cols, *pieces)


def local(sizes, source_embed, target_embed, features, cotangent):
    row_size, col_size = sizes
    emb_count, own = source_embed.shape
    feat = features.shape[1]
    pair = 2 * feat
    depth, width = row_size // 4, col_size // 2
    both = ("row", "col")

    def device(z, y, core, x, skew):
        return (((z % depth) * 2 + y) * 2 + core) * col_size + (x % width) * 2 + (skew ^ y)

    groups = [
        [device(z, y, core, x, skew) for z in range(depth) for y in range(2)]
        for core in range(2) for x in range(width) for skew in range(2)
    ]

    def mate(array, bits):
        return lax.ppermute(array, "col", [(c, c ^ bits) for c in range(col_size)])

    def swap(array):
        return lax.ppermute(array, "row", [(r, r ^ 1) for r in range(row_size)])

    def along_x(array, move, flip):
        pairs = [(x * 2 + y, ((x + move) % width) * 2 + (y ^ flip)) for x in range(width) for y in range(2)]
        return lax.ppermute(array, "col", pairs)

    def along_z(array, move, flip):
        pairs = [
            (device(z, y, core, x, skew), device(z + move, y ^ flip, core, x, skew))
            for z in range(depth) for y in range(2) for core in range(2) for x in range(width) for skew in range(2)
        ]
        return lax.ppermute(array, both, pairs)

    row = lax.broadcasted_iota(jnp.int32, (own + KEPT, pair), 0)
    lane = lax.broadcasted_iota(jnp.int32, (own + KEPT, pair), 1)

    def pack(embed):
        def place(down, right):
            room = ((down, own + KEPT - emb_count - down, 0), (right, pair - own - right, 0))
            return lax.pad(embed, jnp.zeros((), BF16), room)

        total = jnp.pad(features, ((0, KEPT), (0, feat))) + jnp.pad(cotangent, ((0, KEPT), (feat, 0)))
        total = total + place(own, 0)
        for part in range(3):
            top = own + 8 * part
            here = (row >= top) & (row < top + 8) & (lane >= own)
            total = jnp.where(here, place(top - KEPT, own - 64 * part), total)
        return total

    index = lax.axis_index(both)
    place = lax.dynamic_index_in_dim(jnp.asarray(places(row_size, col_size)), index, 0, keepdims=False)
    chunks, alongs = (pack(target_embed), pack(source_embed)), (along_z, along_x)
    near = [jnp.stack([chunk, along(chunk, 0, 1)]) for chunk, along in zip(chunks, alongs)]
    near, place = lax.optimization_barrier((near, place))
    moved = [[along(array, -move, 0) for array, along in zip(near, alongs)] for move in MOVES[1:]]
    b_parts, a_parts = [[array, *[pair[index] for pair in moved]] for index, array in enumerate(near)]
    others = [swap(part) for part in b_parts]
    scaled, stats, kept = row_stats(place, a_parts, b_parts, others, own, feat)
    stats = lax.all_to_all(stats, "col", 0, 0)

    sizes = (own, feat)
    table, mine, *given = weigh(place, stats, scaled, own)
    given = [mate(part, 1) for part in given]
    other_cols, start = tile_sums(place, kept, 1, table, (), (), *sizes, "other_tile")
    other_cols = swap(other_cols)
    own_cols, unused, *pieces, twin = tile_sums(place, kept, 0, table, (start, mine), (), *sizes, "own_tile")
    twin = mate(twin, 1)
    (cols,) = join(join_cols_kernel, "join_cols", [own_cols], own_cols, other_cols, unread=given)
    pieces = join(join_rows_kernel, "join_rows", pieces, *given, twin, *pieces, unread=(cols,))
    cols = lax.all_to_all(cols, both, 0, 0, axis_index_groups=groups)
    pieces = [mate(piece, 2 * slot) if slot else piece for slot, piece in enumerate(pieces)]
    return tuple(finish(cols, pieces, own, feat, emb_count))


def solution(mesh):
    nodes = P(("row", "col"), None)
    embeds = P(None, ("row", "col"))
    sizes = (mesh.shape["row"], mesh.shape["col"])
    return jax.shard_map(
        functools.partial(local, sizes),
        mesh=mesh,
        in_specs=(embeds, embeds, nodes, nodes),
        out_specs=(nodes, nodes, embeds, embeds),
        check_vma=False,
    )
```

```python
import functools

import jax
import jax.numpy as jnp
import numpy as np
from jax import lax
from jax.experimental import pallas as pl
from jax.experimental.pallas import tpu as pltpu
from jax.sharding import PartitionSpec as P

F32 = jnp.float32
BF16 = jnp.bfloat16
LANES = 128
FULL, KEPT = 48, 32
VMEM_MIB = 24
SMEM = pl.BlockSpec(memory_space=pltpu.SMEM)
MOVES = (0, 1, 2, -1)


def pick(total, unit, most):
    size = total
    while size > most or total % size or size % unit:
        size -= unit
    return size


def whole(shape):
    return pl.BlockSpec(shape, lambda *i: (0,) * len(shape))


def shapes(*pairs):
    return [jax.ShapeDtypeStruct(shape, kind) for shape, kind in pairs]


def params(mib=VMEM_MIB):
    return pltpu.CompilerParams(vmem_limit_bytes=mib * 1024 * 1024)


def places(row_size, col_size):
    depth, width = row_size // 4, col_size // 2
    table = np.zeros((row_size * col_size, 16), np.int32)
    for index in range(row_size * col_size):
        row, col = divmod(index, col_size)
        slots = [(col // 2 + move) % width for move in MOVES] + [(row // 4 + move) % depth for move in MOVES]
        table[index, :12] = slots + [col % 2, row // 2 % 2, col, col // 2]
    return table


def fold(block):
    low, high = block[KEPT : KEPT + 8, :LANES], block[KEPT : KEPT + 8, LANES:]
    turned = [pltpu.roll(low, 64, 1), low, pltpu.roll(high, 64, 1), jnp.zeros_like(low)]
    lane = lax.broadcasted_iota(jnp.int32, (KEPT, LANES), 1)
    spare = jnp.where(lane >= 64, jnp.concatenate(turned, axis=0), block[:KEPT, LANES:])
    return jnp.concatenate([block[:KEPT, :LANES], spare], axis=1)


def unfold(block):
    lane = lax.broadcasted_iota(jnp.int32, (KEPT, LANES), 1)
    last = block[:, LANES:]
    spare = jnp.where(lane >= 64, last, 0.0)
    top = jnp.concatenate([block[:, :LANES], jnp.where(lane >= 64, 0.0, last)], axis=1)
    low = pltpu.roll(spare[0:8], 64, 1) + spare[8:16]
    bottom = jnp.concatenate([low, pltpu.roll(spare[16:24], 64, 1)], axis=1)
    return jnp.concatenate([top, bottom, jnp.zeros((FULL - KEPT - 8, block.shape[1]), F32)], axis=0)


def assemble(own, chunk_refs, place_ref, base, parity, pair_ref, turned_ref, nodes_ref):
    even = parity == 0
    blank = jnp.zeros((FULL, 2 * own - chunk_refs[0].shape[2]), F32)
    for slot, chunk_ref in enumerate(chunk_refs):
        start = place_ref[base + slot] * 2 * own
        for flip in range(2):
            rows = pl.ds(pl.multiple_of(start + (parity ^ flip) * own, 64), own)
            pair_ref[rows, :] = chunk_ref[flip, :own, :]
        first = unfold(chunk_ref[0, own:, :].astype(F32))
        second = unfold(chunk_ref[1, own:, :].astype(F32))
        left = jnp.concatenate([jnp.where(even, first, second), blank], axis=1)
        right = jnp.concatenate([blank, jnp.where(even, second, first)], axis=1)
        both = left + pltpu.roll(right, own - blank.shape[1], 1)
        turned_ref[:FULL, pl.ds(pl.multiple_of(start, LANES), 2 * own)] = both.astype(BF16)
    turned_ref[FULL:, :] = jnp.zeros((LANES - FULL, turned_ref.shape[1]), BF16)
    nodes_ref[...] = jnp.transpose(turned_ref[...])


def stats_kernel(own, feat, place_ref, *rest):
    parts = len(MOVES)
    a_refs, b0_refs, b1_refs = rest[0 : 2 * parts : 2], rest[1 : 2 * parts : 2], rest[2 * parts : 3 * parts]
    scaled_ref, stats_ref, a_pair, a_pair_t, a_src, a_src_t, b_pair, b_dst, b_dst_t, scores, peaks = rest[3 * parts :]
    step = pl.program_id(0)
    last = pl.num_programs(0) - 1
    count, cols = scores.shape
    span = pick(cols, LANES, 512)
    repeat = span // LANES

    def tiles(array):
        return [array[:, lane : lane + LANES] for lane in range(0, span, LANES)]

    def work(ahead, behind):
        block = step - 1 if behind else step
        here = pl.ds(pl.multiple_of(block * count, count), count)
        there = pl.ds(pl.multiple_of(step * count, count), count)
        total = jnp.zeros((count, LANES), F32)
        peak = jnp.zeros((count, LANES), F32)
        sums = jnp.zeros((count, 2 * feat), F32)
        for start in range(0, cols, span):
            part = slice(start, start + span)
            if behind:
                before = peaks[...]
                half = jnp.exp(scores[:, part] - jnp.concatenate([before] * repeat, axis=1)).astype(BF16)
                total = total + sum(tiles(half.astype(F32)))
                sums = sums + jnp.dot(half, b_pair[part, :], preferred_element_type=F32)
            if ahead:
                fresh = jnp.maximum(jnp.dot(a_src[there, :], b_dst_t[:, part], preferred_element_type=F32), 0.0)
                scores[:, part] = fresh
                peak = functools.reduce(jnp.maximum, tiles(fresh), peak)
        if behind:
            total = jnp.sum(total, axis=1, keepdims=True)
            sums = sums / total
            scaled_ref[...] = sums.astype(BF16)
            mates = a_pair[here, :].astype(F32)
            inner = jnp.sum(sums[:, :feat] * mates[:, feat:] + sums[:, feat:] * mates[:, :feat], axis=1, keepdims=True)
            lane = lax.broadcasted_iota(jnp.int32, (count, LANES), 1)
            table = jnp.where(lane == 0, peaks[...], jnp.where(lane == 1, total, inner))
            stats_ref[...] = jnp.broadcast_to(jnp.transpose(table)[:4][None], stats_ref.shape)
        if ahead:
            peaks[...] = jnp.broadcast_to(jnp.max(peak, axis=1, keepdims=True), peaks.shape)

    @pl.when(step == 0)
    def _():
        assemble(own, a_refs, place_ref, 0, place_ref[8], a_pair, a_src_t, a_src)
        half = b_pair.shape[0] // 2
        for index, b_refs in enumerate((b0_refs, b1_refs)):
            part = pl.ds(index * half, half)
            outs = (b_pair.at[part, :], b_dst_t.at[:, part], b_dst.at[part, :])
            assemble(own, b_refs, place_ref, 4, place_ref[9], *outs)
        a_pair_t[:feat] = jnp.transpose(a_pair[:, feat:])
        a_pair_t[feat:] = jnp.transpose(a_pair[:, :feat])
        work(True, False)

    @pl.when((step > 0) & (step < last))
    def _():
        work(True, True)

    @pl.when(step == last)
    def _():
        work(False, True)


def row_stats(place, a_parts, b0_parts, b1_parts, own, feat):
    mates = sum(part.shape[0] for part in a_parts)
    rows = mates * own
    cols = 2 * own * sum(part.shape[0] for part in b0_parts)
    pair = 2 * feat
    step = pick(rows, LANES, 768)
    kept = [((rows, pair), BF16), ((pair, rows), BF16), ((rows, LANES), BF16), ((LANES, rows), BF16)]
    kept += [((cols, pair), BF16), ((cols, LANES), BF16), ((LANES, cols), BF16)]
    parts = [part for both in zip(a_parts, b0_parts) for part in both] + b1_parts
    scaled, stats, *kept = pl.pallas_call(
        functools.partial(stats_kernel, own, feat),
        grid=(rows // step + 1,),
        in_specs=[SMEM] + [whole(x.shape) for x in parts],
        out_specs=[
            pl.BlockSpec((step, pair), lambda i: (jnp.maximum(i - 1, 0), 0)),
            pl.BlockSpec((mates, 4, step), lambda i: (0, 0, jnp.maximum(i - 1, 0))),
        ]
        + [whole(shape) for shape, kind in kept],
        out_shape=shapes(((rows, pair), BF16), ((mates, 4, rows), F32), *kept),
        scratch_shapes=[pltpu.VMEM((step, cols), F32), pltpu.VMEM((step, LANES), F32)],
        compiler_params=params(),
        cost_estimate=pl.CostEstimate(flops=2 * rows * cols * 512, bytes_accessed=8 << 20, transcendentals=rows * cols),
        name="row_stats",
    )(place, *parts)
    return scaled, stats, kept


def weigh_kernel(own, place_ref, stats_ref, scaled_ref, table_ref, mine_ref, given_ref, weights_ref):
    stats = stats_ref[...]
    peaks = stats[:, 0:1]
    peak = jnp.max(peaks, axis=0)
    weights = jnp.exp(peaks - peak[None]) * stats[:, 1:2]
    total = jnp.sum(weights, axis=0)
    table_ref[0:1, :] = peak + jnp.log(total)
    table_ref[1:2, :] = jnp.sum(weights * stats[:, 2:3], axis=0) / total
    table_ref[2:, :] = jnp.zeros((table_ref.shape[0] - 2, table_ref.shape[1]), F32)
    at = place_ref[10]
    weight = jnp.exp(stats_ref[at, 0:1] - peak) * stats_ref[at, 1:2] / total
    weights_ref[...] = jnp.transpose(jnp.broadcast_to(weight, (LANES, weight.shape[1])))
    for slot in range(mine_ref.shape[0]):
        for flip, out_ref in enumerate((mine_ref, given_ref)):
            chunk = 2 * (place_ref[11] ^ slot) + (place_ref[8] ^ flip)
            rows = pl.ds(pl.multiple_of(chunk * own, 64), own)
            out_ref[slot] = (weights_ref[rows, 0:1] * scaled_ref[rows, :].astype(F32)).astype(BF16)


def weigh(place, stats, scaled, own):
    rows, pair = scaled.shape
    count = stats.shape[0] // 2
    part = ((count, own, pair), BF16)
    return pl.pallas_call(
        functools.partial(weigh_kernel, own),
        in_specs=[SMEM] + [pl.BlockSpec(memory_space=pltpu.VMEM)] * 2,
        out_shape=shapes(((8, rows), F32), part, part),
        scratch_shapes=[pltpu.VMEM((rows, LANES), F32)],
        compiler_params=params(8),
        name="weigh",
    )(place, stats, scaled)


def tile_kernel(own, feat, half, place_ref, a_pair, a_pair_t, a_src, a_src_t, b_pair, b_dst, b_dst_t, table, *rest):
    pair = 2 * feat
    last = half == 0
    if last:
        start_ref, mine_ref, cols_ref, source_ref, *piece_refs, twin_ref = rest[:-5]
        col_sums, target_sums, scores, outer, slots = rest[-5:]
    else:
        cols_ref, source_ref, col_sums, target_sums, scores, outer = rest
    rows = a_pair.shape[0]
    cols = col_sums.shape[0]
    span = scores.shape[2]
    here = slice(half * cols, (half + 1) * cols)

    def ahead(index):
        part = slice(index * span, (index + 1) * span)
        scores[index % 2] = jnp.dot(b_dst[here, :], a_src_t[:, part], preferred_element_type=F32)
        outer[index % 2] = jnp.dot(b_pair[here, :], a_pair_t[:, part], preferred_element_type=F32)

    def behind(index):
        part = slice(index * span, (index + 1) * span)
        score = scores[index % 2]
        soft = jnp.exp(jnp.maximum(score, 0.0) - table[0:1, part])
        grad = jnp.where(score > 0.0, soft * (outer[index % 2] - table[1:2, part]), 0.0)
        soft_half = soft.astype(BF16)
        grad_half = grad.astype(BF16)
        more_cols = jnp.dot(soft_half, a_pair[part, :], preferred_element_type=F32)
        more_target = jnp.dot(grad_half, a_src[part, :], preferred_element_type=F32)
        more_source = jnp.dot(b_dst_t[:FULL, here], grad_half, preferred_element_type=F32)
        col_sums[...] = col_sums[...] + more_cols if index else more_cols
        target_sums[...] = target_sums[...] + more_target if index else more_target
        source_ref[:, part] = start_ref[:, part] + more_source if last else more_source

    count = rows // span
    ahead(0)
    for index in range(count):
        if index + 1 < count:
            ahead(index + 1)
        behind(index)
    for slot in range(cols_ref.shape[0]):
        chunk = slice(slot * own, (slot + 1) * own)
        cols_ref[slot, :own, :] = col_sums[chunk, :].astype(BF16)
        wide = jnp.concatenate([target_sums[chunk, :], jnp.zeros((pair - own, LANES), F32)], axis=0)
        cols_ref[slot, own:, :] = fold(jnp.transpose(wide)[:FULL]).astype(BF16)
    if last:
        fill = jnp.zeros((FULL, pair - own), F32)
        for chunk in range(slots.shape[0]):
            part = source_ref[:, chunk * own : (chunk + 1) * own]
            slots[place_ref[10] ^ chunk] = fold(jnp.concatenate([part, fill], axis=1))
        for slot, piece_ref in enumerate(piece_refs):
            piece_ref[:own, :] = mine_ref[slot]
            piece_ref[own:, :] = slots[2 * slot].astype(BF16)
            twin_ref[slot] = slots[2 * slot + 1].astype(BF16)


def tile_sums(place, kept, half, table, late, unread, own, feat, name):
    rows, pair = kept[0].shape
    cols = kept[4].shape[0] // 2
    mates = rows // own
    span = pick(rows, LANES, 256)
    scratch = [pltpu.VMEM((cols, pair), F32), pltpu.VMEM((cols, LANES), F32)] + [pltpu.VMEM((2, cols, span), F32)] * 2
    kinds = []
    if half == 0:
        kinds = [((own + KEPT, pair), BF16)] * (mates // 2) + [((mates // 2, KEPT, pair), BF16)]
        scratch += [pltpu.VMEM((mates, KEPT, pair), F32)]
    vmem, anywhere = pl.BlockSpec(memory_space=pltpu.VMEM), pl.BlockSpec(memory_space=pl.ANY)
    work = 1 << 20 if half == 0 else 2 * rows * cols * 1280
    return pl.pallas_call(
        functools.partial(tile_kernel, own, feat, half),
        in_specs=[SMEM] + [vmem] * (len(kept) + 1 + len(late)) + [anywhere] * len(unread),
        out_shape=shapes(((cols // own, own + KEPT, pair), BF16), ((FULL, rows), F32), *kinds),
        scratch_shapes=scratch,
        compiler_params=params(),
        cost_estimate=pl.CostEstimate(flops=work, bytes_accessed=1 << 20, transcendentals=work >> 11),
        name=name,
    )(place, *kept, table, *late, *unread)


def join_cols_kernel(own_ref, other_ref, unread_ref, out_ref):
    out_ref[...] = (own_ref[...].astype(F32) + other_ref[...].astype(F32)).astype(BF16)


def join_rows_kernel(given_ref, twin_ref, *rest):
    count, own = given_ref.shape[:2]
    for slot, (piece_ref, out_ref) in enumerate(zip(rest[:count], rest[count + 1 :])):
        out_ref[:own, :] = (piece_ref[:own, :].astype(F32) + given_ref[slot].astype(F32)).astype(BF16)
        out_ref[own:, :] = (piece_ref[own:, :].astype(F32) + twin_ref[slot].astype(F32)).astype(BF16)


def join(kernel, name, outs, *arrays, unread=()):
    vmem, anywhere = pl.BlockSpec(memory_space=pltpu.VMEM), pl.BlockSpec(memory_space=pl.ANY)
    return pl.pallas_call(
        kernel,
        in_specs=[vmem] * len(arrays) + [anywhere] * len(unread),
        out_shape=[jax.ShapeDtypeStruct(out.shape, out.dtype) for out in outs],
        compiler_params=params(8),
        name=name,
    )(*arrays, *unread)


def finish_kernel(own, feat, emb_count, cols_ref, *rest):
    piece_refs, (hop_ref, grad_ref, source_ref, target_ref) = rest[:-4], rest[-4:]
    total = jnp.zeros((own, 2 * feat), F32)
    extra = jnp.zeros((cols_ref.shape[1] - own, 2 * feat), F32)
    source = extra
    for piece_ref in piece_refs:
        total = total + piece_ref[:own, :].astype(F32)
        source = source + piece_ref[own:, :].astype(F32)
    for slot in range(cols_ref.shape[0]):
        total = total + cols_ref[slot, :own, :].astype(F32)
        extra = extra + cols_ref[slot, own:, :].astype(F32)
    hop_ref[...] = total[:, :feat].astype(BF16)
    grad_ref[...] = total[:, feat:].astype(BF16)
    source_ref[...] = unfold(source)[:emb_count, :own]
    target_ref[...] = unfold(extra)[:emb_count, :own]


def finish(cols, pieces, own, feat, emb_count):
    return pl.pallas_call(
        functools.partial(finish_kernel, own, feat, emb_count),
        out_shape=shapes(
            ((own, feat), BF16), ((own, feat), BF16), ((emb_count, own), F32), ((emb_count, own), F32)
        ),
        compiler_params=params(8),
        name="finish",
    )(cols, *pieces)


def local(sizes, source_embed, target_embed, features, cotangent):
    row_size, col_size = sizes
    emb_count, own = source_embed.shape
    feat = features.shape[1]
    pair = 2 * feat
    depth, width = row_size // 4, col_size // 2
    both = ("row", "col")

    def device(z, y, core, x, skew):
        return (((z % depth) * 2 + y) * 2 + core) * col_size + (x % width) * 2 + (skew ^ y)

    groups = [
        [device(z, y, core, x, skew) for z in range(depth) for y in range(2)]
        for core in range(2) for x in range(width) for skew in range(2)
    ]

    def mate(array, bits):
        return lax.ppermute(array, "col", [(c, c ^ bits) for c in range(col_size)])

    def swap(array):
        return lax.ppermute(array, "row", [(r, r ^ 1) for r in range(row_size)])

    def along_x(array, move, flip):
        pairs = [(x * 2 + y, ((x + move) % width) * 2 + (y ^ flip)) for x in range(width) for y in range(2)]
        return lax.ppermute(array, "col", pairs)

    def along_z(array, move, flip):
        pairs = [
            (device(z, y, core, x, skew), device(z + move, y ^ flip, core, x, skew))
            for z in range(depth) for y in range(2) for core in range(2) for x in range(width) for skew in range(2)
        ]
        return lax.ppermute(array, both, pairs)

    row = lax.broadcasted_iota(jnp.int32, (own + KEPT, pair), 0)
    lane = lax.broadcasted_iota(jnp.int32, (own + KEPT, pair), 1)

    def pack(embed):
        def place(down, right):
            room = ((down, own + KEPT - emb_count - down, 0), (right, pair - own - right, 0))
            return lax.pad(embed, jnp.zeros((), BF16), room)

        total = jnp.pad(features, ((0, KEPT), (0, feat))) + jnp.pad(cotangent, ((0, KEPT), (feat, 0)))
        total = total + place(own, 0)
        for part in range(3):
            top = own + 8 * part
            here = (row >= top) & (row < top + 8) & (lane >= own)
            total = jnp.where(here, place(top - KEPT, own - 64 * part), total)
        return total

    index = lax.axis_index(both)
    place = lax.dynamic_index_in_dim(jnp.asarray(places(row_size, col_size)), index, 0, keepdims=False)
    chunks, alongs = (pack(target_embed), pack(source_embed)), (along_z, along_x)
    near = [jnp.stack([chunk, along(chunk, 0, 1)]) for chunk, along in zip(chunks, alongs)]
    near, place = lax.optimization_barrier((near, place))
    moved = [[along(array, -move, 0) for array, along in zip(near, alongs)] for move in MOVES[1:]]
    b_parts, a_parts = [[array, *[pair[index] for pair in moved]] for index, array in enumerate(near)]
    others = [swap(part) for part in b_parts]
    scaled, stats, kept = row_stats(place, a_parts, b_parts, others, own, feat)
    stats = lax.all_to_all(stats, "col", 0, 0)

    sizes = (own, feat)
    table, mine, *given = weigh(place, stats, scaled, own)
    given = [mate(part, 1) for part in given]
    other_cols, start = tile_sums(place, kept, 1, table, (), (), *sizes, "other_tile")
    other_cols = swap(other_cols)
    own_cols, unused, *pieces, twin = tile_sums(place, kept, 0, table, (start, mine), (), *sizes, "own_tile")
    twin = mate(twin, 1)
    (cols,) = join(join_cols_kernel, "join_cols", [own_cols], own_cols, other_cols, unread=given)
    pieces = join(join_rows_kernel, "join_rows", pieces, *given, twin, *pieces, unread=(cols,))
    cols = lax.all_to_all(cols, both, 0, 0, axis_index_groups=groups)
    pieces = [mate(piece, 2 * slot) if slot else piece for slot, piece in enumerate(pieces)]
    return tuple(finish(cols, pieces, own, feat, emb_count))


def solution(mesh):
    nodes = P(("row", "col"), None)
    embeds = P(None, ("row", "col"))
    sizes = (mesh.shape["row"], mesh.shape["col"])
    return jax.shard_map(
        functools.partial(local, sizes),
        mesh=mesh,
        in_specs=(embeds, embeds, nodes, nodes),
        out_specs=(nodes, nodes, embeds, embeds),
        check_vma=False,
    )
```
